32 devices in a mesh: grp: 2 (over x), tok: 16 (over z, y, core).
Axes of the slice: x: 2, y: 2, z: 4, core: 2. Of those that a mesh axis runs over, the one named last changes fastest.
Arguments:
- frames: bfloat16 [256, 48, 4096], P(('grp', 'tok')), parts along dimension 0, may hold values from -6 to 6
- clip_lengths: int32 [8], P('grp'), parts along dimension 0, may hold values from 1 to 56, as said below
- sequence_slot_map: int32 [2048], P(('grp', 'tok')), parts along dimension 0, may hold values from 0 to 1023, as said below
- stem_weight: bfloat16 [128, 48], replicated, may hold values from -0.875 to 0.875
- time_weight: bfloat16 [3, 128, 128], replicated, may hold values from -0.3125 to 0.3125
- norm_gain: float32 [128], replicated, may hold values from 0.1 to 1.9
- mid_weight: bfloat16 [512, 2048], replicated, may hold values from -0.125 to 0.125
- latent_weight: bfloat16 [16, 4096], replicated, may hold values from -0.09375 to 0.09375
- patch_embed_weight: bfloat16 [64, 2048], replicated, may hold values from -0.75 to 0.75
Outputs:
- dit_rows: bfloat16 [2048, 2048], P(('grp', 'tok')), parts along dimension 0
The draws below stay inside these ranges and needn't reach their ends.
There are 2 independent parts, one for each index of `grp`. The reference program is written for one: setup_inputs(seed, part) draws one part's arguments, and reference() takes and returns one part's arrays. A program takes and returns all parts, laid end to end along the dimension named above; an argument that names none is the same for every part. Nothing has to cross between parts.
Inputs may be any that keep to these rules, and one draw needn't show every extreme that they name: `clip_lengths`: clips fill the 16 slabs in order: the counts ceil(length / 8) sum to 16. `sequence_slot_map`: A permutation of the 1024 sequence slots. The rows of one slab send at most 8 rows to the slots of any one slab (exactly 8 to some), and how many slab s sends to slab (s + k) mod 16 depends on k only.
All inputs are finite; a program needn't handle non-finite values.
Results may differ from the reference program's by a relative error of at most 0.0071.
Values may be sent and summed in bfloat16 or wider, within the bound.
A program may use at most 128 MiB of HBM per device.

```python
import jax
import jax.numpy as jnp
from jax import lax

CIN = 48
C1 = 128
C2 = 512
LATC = 16
DIFFUSION_WIDTH = 2048
FRAMES = 8
LS = 16
POS = 4096
PATCH_FEATURES = 64
SLAB_ROW_COUNT = 64
CAP = 8
CLIPS = 4
TFRAMES = 128
N_TOK = 16


def draw_clip_lengths(key, part):
    keys = jax.random.split(jax.random.fold_in(key, 11), 3)
    order = jax.random.permutation(keys[0], CLIPS).astype(jnp.int32)
    pairs = CLIPS // 2
    moved = jax.random.randint(keys[1], (pairs,), 0, 4).astype(jnp.int32)
    moved = moved.at[0].set(3)
    counts = jnp.full((CLIPS,), 4, jnp.int32)
    counts = counts.at[order[0:2 * pairs:2]].add(moved)
    counts = counts.at[order[1:2 * pairs:2]].add(-moved)
    tails = jax.random.randint(keys[2], (CLIPS,), 1, 9).astype(jnp.int32)
    tails = tails.at[order[0]].set(8)
    tails = tails.at[order[1]].set(1)
    return (8 * (counts - 1) + tails).astype(jnp.int32)


def draw_sequence_slot_map(key, part):
    keys = jax.random.split(jax.random.fold_in(key, 23), 4)
    rest = jax.random.permutation(keys[0], N_TOK * CAP - CAP) + CAP
    chosen = jnp.concatenate([jnp.arange(CAP, dtype=jnp.int32), rest[:SLAB_ROW_COUNT - CAP].astype(jnp.int32)])
    groups = jnp.sort(chosen) // CAP
    offsets = jax.random.permutation(keys[1], N_TOK).astype(jnp.int32)
    slab_ids = jnp.arange(N_TOK, dtype=jnp.int32)
    arrival = jax.vmap(lambda s: jax.random.permutation(jax.random.fold_in(keys[3], s), SLAB_ROW_COUNT))(slab_ids).astype(jnp.int32)
    slot_position = jnp.arange(SLAB_ROW_COUNT, dtype=jnp.int32)

    def one_source(source):
        order = jax.random.permutation(jax.random.fold_in(keys[2], source), SLAB_ROW_COUNT)
        target = (source + offsets[groups]) % N_TOK
        slots = target * SLAB_ROW_COUNT + arrival[target, slot_position]
        return jnp.zeros((SLAB_ROW_COUNT,), jnp.int32).at[order].set(slots.astype(jnp.int32))
    return jax.vmap(one_source)(slab_ids).reshape(N_TOK * SLAB_ROW_COUNT)


def block_scale(stream_key, shape, cuts, smallest, top_value):
    def one(position, blocks):
        steps = jax.random.uniform(jax.random.fold_in(jax.random.fold_in(stream_key, 6), position), (blocks,), jnp.float32, smallest / len(cuts), top_value / len(cuts))
        return jnp.repeat(jnp.exp(steps), shape[position] // blocks).reshape((-1,) + (1,) * (len(shape) - position - 1))

    level = one(*cuts[0])
    for cut in cuts[1:]:
        level = level * one(*cut)
    return level


def gaussian(key, dims, scale, reach, shards=(), kind=jnp.bfloat16):
    entries = scale * jax.random.normal(key, dims, jnp.float32)
    if shards:
        entries = entries * block_scale(key, dims, shards, -0.22, 0.18)
    return jnp.clip(entries, -reach, reach).astype(kind)


def setup_inputs(seed: int = 0, part: int = 0) -> dict:
    key_list = jax.random.split(jax.random.key(seed), 10)
    part_keys = jax.random.split(jax.random.fold_in(key_list[9], part), 10)
    return {
        "frames": gaussian(part_keys[0], (TFRAMES, CIN, POS), 1.0, 6.0, ((0, 16),)),
        "clip_lengths": draw_clip_lengths(jax.random.fold_in(jax.random.fold_in(key_list[9], part), 71), part),
        "sequence_slot_map": draw_sequence_slot_map(jax.random.fold_in(jax.random.fold_in(key_list[9], part), 71), part),
        "stem_weight": gaussian(key_list[3], (C1, CIN), CIN ** -0.5, 0.875),
        "time_weight": gaussian(key_list[4], (3, C1, C1), (3 * C1) ** -0.5, 0.3125),
        "norm_gain": jnp.clip(1.0 + 0.18 * jax.random.normal(key_list[5], (C1,), jnp.float32), 0.1, 1.9),
        "mid_weight": gaussian(key_list[6], (C2, C1 * 16), (C1 * 16) ** -0.5, 0.125),
        "latent_weight": gaussian(key_list[7], (LATC, FRAMES * C2), (FRAMES * C2) ** -0.5, 0.09375),
        "patch_embed_weight": gaussian(key_list[8], (PATCH_FEATURES, DIFFUSION_WIDTH), PATCH_FEATURES ** -0.5, 0.75),
    }


def project(weight, data):
    return jnp.einsum('oc,fcp->fop', weight.astype(jnp.float32), data.astype(jnp.float32))

def encode(slab_frames, prior_frames, valid, keep, stem_weight, time_weight, norm_gain, mid_weight, latent_weight):
    first_section = (project(stem_weight, slab_frames) * valid[:, None, None]).astype(jnp.bfloat16)
    prior = (project(stem_weight, prior_frames) * keep).astype(jnp.bfloat16)
    joined = jnp.concatenate([prior, first_section], axis=0)
    mixed = project(time_weight[0], joined[2:10])
    mixed = mixed + project(time_weight[1], joined[1:9])
    mixed = mixed + project(time_weight[2], joined[0:8])
    meansq = lax.optimization_barrier(jnp.mean(mixed * mixed, axis=1, keepdims=True))
    normed = mixed * lax.rsqrt(meansq + 1e-06) * norm_gain.astype(jnp.float32)[None, :, None]
    activated = (normed * jax.nn.sigmoid(normed)).astype(jnp.bfloat16)
    regrouped = activated.reshape(FRAMES, C1 * 16, LS * LS)
    deep = project(mid_weight, regrouped)
    deep = (deep * jax.nn.sigmoid(deep)).astype(jnp.bfloat16)
    taps = latent_weight.astype(jnp.float32).reshape(LATC, FRAMES, C2)
    latent = jnp.einsum('ofc,fcp->op', taps, deep.astype(jnp.float32)).astype(jnp.bfloat16)
    half = LS // 2
    return latent.reshape(LATC, half, 2, half, 2).transpose(1, 3, 0, 2, 4).reshape(half * half, LATC * 4)

def reference(frames, clip_lengths, sequence_slot_map, stem_weight, time_weight, norm_gain, mid_weight, latent_weight, patch_embed_weight):
    counts = (clip_lengths + 7) // 8
    ends = jnp.cumsum(counts)
    starts = ends - counts
    clip_ids = jnp.arange(CLIPS, dtype=jnp.int32)

    def one_slab(slab):
        which = jnp.sum((ends <= slab).astype(jnp.int32))
        hot = clip_ids == which
        start = jnp.sum(jnp.where(hot, starts, 0))
        length = jnp.sum(jnp.where(hot, clip_lengths, 0))
        live = jnp.clip(length - FRAMES * (slab - start), 0, FRAMES)
        valid = (jnp.arange(FRAMES, dtype=jnp.int32) < live).astype(jnp.float32)
        keep = jnp.where(slab == start, jnp.float32(0.0), jnp.float32(1.0))
        here = lax.dynamic_slice_in_dim(frames, (slab * FRAMES).astype(jnp.int32), FRAMES, 0)
        before = lax.dynamic_slice_in_dim(frames, jnp.maximum(slab * FRAMES - 2, 0).astype(jnp.int32), 2, 0)
        return encode(here, before, valid, keep, stem_weight, time_weight, norm_gain, mid_weight, latent_weight)
    rows = lax.map(one_slab, jnp.arange(N_TOK, dtype=jnp.int32)).reshape(N_TOK * SLAB_ROW_COUNT, LATC * 4)
    embedded_tokens = jnp.dot(rows, patch_embed_weight, preferred_element_type=jnp.float32).astype(jnp.bfloat16)
    return jnp.zeros((N_TOK * SLAB_ROW_COUNT, DIFFUSION_WIDTH), jnp.bfloat16).at[sequence_slot_map].set(embedded_tokens)
```

```python
import functools

import jax
import jax.numpy as jnp
from jax import lax
from jax.experimental import pallas as pl
from jax.experimental.pallas import tpu as pltpu
from jax.sharding import PartitionSpec as P

F32 = jnp.float32
BF16 = jnp.bfloat16
I32 = jnp.int32
SPAN = 3


def iota(shape, dim):
    return lax.broadcasted_iota(I32, shape, dim)


def dot(a, b, contract=((1,), (0,))):
    return lax.dot_general(a, b, (contract, ((), ())), preferred_element_type=F32)


def shift_of(size):
    assert size & (size - 1) == 0
    return size.bit_length() - 1


def kernel(
    n, side, clip_ref, slot_hbm, gain_hbm, frames_hbm, stem_hbm, time_hbm, mid_hbm, lat_hbm, pe_hbm,
    out_ref,
    slot, gain, frames, stem, time, mid, lat, pe,
    toeplitz, masked, wide_gain, mid_perm, pe_perm, select, s_ref, outbuf, inbuf,
    load_sem, carry_sems, send_sem, recv_sem,
):
    me = lax.axis_index("tok")
    nframes, cin, _ = frames_hbm.shape
    c1 = stem_hbm.shape[0]
    cells = side * side
    blocks = frames_hbm.shape[2] // cells
    c2 = mid_hbm.shape[0]
    latc = lat_hbm.shape[0]
    rows = slot_hbm.shape[1]
    cap = outbuf.shape[1]
    width = outbuf.shape[2]
    slots = n * cap
    features = pe_hbm.shape[0]
    quads = features // latc

    loads = [
        pltpu.make_async_copy(stem_hbm, stem, load_sem.at[0]),
        pltpu.make_async_copy(time_hbm, time, load_sem.at[1]),
        pltpu.make_async_copy(gain_hbm, gain, load_sem.at[2]),
        pltpu.make_async_copy(frames_hbm.at[0:5], frames.at[2:7], load_sem.at[3]),
        pltpu.make_async_copy(mid_hbm, mid, load_sem.at[4]),
        pltpu.make_async_copy(slot_hbm, slot, load_sem.at[5]),
        pltpu.make_async_copy(frames_hbm.at[5:nframes], frames.at[7 : nframes + 2], load_sem.at[6]),
        pltpu.make_async_copy(pe_hbm, pe, load_sem.at[7]),
    ] + [
        pltpu.make_async_copy(lat_hbm.at[:, f * c2 : (f + 1) * c2], lat.at[f], load_sem.at[8 + f])
        for f in range(nframes)
    ]
    for load in loads:
        load.start()

    barrier = pltpu.get_barrier_semaphore()

    def greet(k, _):
        pl.semaphore_signal(
            barrier, inc=1, device_id={"tok": lax.rem(me + k, n)}, device_id_type=pl.DeviceIdType.MESH
        )
        return 0

    lax.fori_loop(1, n, greet, 0)
    pl.semaphore_wait(barrier, n - 1)

    carry = pltpu.make_async_remote_copy(
        src_ref=frames_hbm.at[nframes - 2 : nframes],
        dst_ref=frames.at[0:2],
        send_sem=carry_sems.at[0],
        recv_sem=carry_sems.at[1],
        device_id={"tok": lax.rem(me + 1, n)},
        device_id_type=pl.DeviceIdType.MESH,
    )

    @pl.when(me < n - 1)
    def _():
        carry.start()

    @pl.when(me == 0)
    def _():
        frames[0:2] = jnp.zeros_like(frames[0:2])

    start = jnp.int32(0)
    end = jnp.int32(0)
    live = jnp.int32(0)
    keep = jnp.float32(1.0)
    for c in range(clip_ref.shape[0]):
        length = clip_ref[c]
        start = end
        end = end + lax.div(length + (nframes - 1), jnp.int32(nframes))
        inside = jnp.logical_and(start <= me, me < end)
        live = jnp.where(inside, jnp.clip(length - nframes * (me - start), 0, nframes), live)
        keep = jnp.where(jnp.logical_and(inside, start == me), jnp.float32(0.0), keep)

    kspan = (SPAN + 2) * cin
    loads[0].wait()
    loads[1].wait()
    placed_stem = [
        dot(stem[...], (iota((cin, kspan), 1) == iota((cin, kspan), 0) + b * cin).astype(BF16)).astype(BF16)
        for b in range(SPAN + 2)
    ]
    for j in range(SPAN):
        row = dot(time[2], placed_stem[j]) + dot(time[1], placed_stem[j + 1]) + dot(time[0], placed_stem[j + 2])
        toeplitz[j * c1 : (j + 1) * c1, :] = row.astype(BF16)

    loads[2].wait()
    diagonal = iota((c1, c1), 0) == iota((c1, c1), 1)
    column = jnp.sum(jnp.where(diagonal, jnp.broadcast_to(gain[...], (c1, c1)), 0.0), axis=1, keepdims=True)
    wide_gain[...] = jnp.broadcast_to(0.5 * column, wide_gain.shape)

    loads[4].wait()
    chunk = 16 * blocks
    k_in, k_out = iota((chunk, chunk), 0), iota((chunk, chunk), 1)
    bits = shift_of(blocks)
    swap = ((k_in >> bits) == (k_out & 15)) & ((k_in & (blocks - 1)) == (k_out >> 4))
    swap = swap.astype(BF16)
    for q in range(c1 // 16):
        at = slice(q * chunk, (q + 1) * chunk)
        mid_perm[:, at] = dot(mid[:, at], swap).astype(BF16)

    loads[5].wait()
    row_bits = shift_of(rows)
    where_to = slot[...]
    target = where_to >> row_bits
    place = where_to & (rows - 1)
    onehot = iota((n, rows), 0) == target
    before = (iota((rows, rows), 0) < iota((rows, rows), 1)).astype(BF16)
    earlier = dot(onehot.astype(BF16), before)
    rank = jnp.sum(jnp.where(onehot, earlier, 0.0), axis=0, keepdims=True).astype(I32)
    select[...] = (iota((slots, rows), 0) == target * cap + rank).astype(BF16)

    loads[7].wait()
    f_out, f_in = iota((width, features), 0), iota((width, features), 1)
    latc_bits, quad_bits = shift_of(latc), shift_of(quads)
    reorder = (f_out >> latc_bits == (f_in & (quads - 1))) & ((f_out & (latc - 1)) == f_in >> quad_bits)
    pe_perm[...] = dot(reorder.astype(BF16), pe[...]).astype(BF16)

    for f in range(nframes):
        loads[8 + f].wait()

    def group(first, count, latent):
        column_id = iota((1, kspan), 1)
        on = jnp.where(column_id < cin * (live - first + 2), jnp.float32(1.0), jnp.float32(0.0))
        on = jnp.where(column_id < cin * (2 - first), keep, on)
        masked[...] = (toeplitz[...].astype(F32) * on).astype(BF16)
        m_rows, k_rows = count * c1, (count + 2) * cin

        def conv(ab, _):
            at = pl.ds(pl.multiple_of(ab * cells, cells), cells)
            data = frames[first : first + count + 2, :, at].reshape(k_rows, cells)
            h = dot(masked[0:m_rows, 0:k_rows], data)
            for j in range(count):
                hj = h[j * c1 : (j + 1) * c1]
                scale = lax.rsqrt(jnp.sum(hj * hj, axis=0, keepdims=True) * (1.0 / c1) + 1e-6)
                x = hj * scale * wide_gain[...]
                u = x + x * jnp.tanh(x)
                s_ref[j, :, ab] = u.astype(BF16).reshape(c1 // 16, 16, cells)
            return 0

        lax.fori_loop(0, blocks, conv, 0, unroll=2)

        def deep(j, acc):
            g = 0.5 * dot(mid_perm[...], s_ref[j].reshape(c1 * blocks, cells))
            m = (g + g * jnp.tanh(g)).astype(BF16)
            return acc + dot(lat[first + j], m)

        return lax.fori_loop(0, count, deep, latent)

    latent = jnp.zeros((latc, cells), F32)
    loads[3].wait()
    latent = group(2, 3, latent)
    loads[6].wait()
    latent = group(5, 3, latent)

    @pl.when(me > 0)
    def _():
        carry.wait_recv()

    latent = group(0, 2, latent)

    half = side // 2
    half_bits = shift_of(half)
    cell, row_id = iota((cells, rows), 0), iota((cells, rows), 1)
    latent = latent.astype(BF16)
    parts = []
    for q in range(quads):
        a, b = q // 2, q % 2
        pick = cell == (2 * (row_id >> half_bits) + a) * side + 2 * (row_id & (half - 1)) + b
        parts.append(dot(latent, pick.astype(BF16)))
    tag = jnp.where(iota((width - features, rows), 0) == 0, (place + 1).astype(F32), 0.0)
    rows_t = jnp.concatenate(parts + [tag], axis=0).astype(BF16)
    payload = dot(select[...], rows_t, ((1,), (1,)))
    outbuf[...] = payload.reshape(n, cap, width)

    def exchange(k):
        to = lax.rem(me + k, n)
        return pltpu.make_async_remote_copy(
            src_ref=outbuf.at[to],
            dst_ref=inbuf.at[me],
            send_sem=send_sem.at[k],
            recv_sem=recv_sem.at[k],
            device_id={"tok": to},
            device_id_type=pl.DeviceIdType.MESH,
        )

    def send(k, _):
        exchange(k).start()
        return 0

    def finish(k, _):
        exchange(k).wait()
        return 0

    lax.fori_loop(1, n, send, 0)
    inbuf[me] = outbuf[me]
    lax.fori_loop(1, n, finish, 0)

    arrived = inbuf[...].reshape(slots, width)
    arrange = (arrived[:, features : features + 1] == (iota((slots, rows), 1) + 1).astype(F32)).astype(BF16)
    placed = dot(arrange, arrived.astype(BF16), ((0,), (0,))).astype(BF16)
    out_ref[...] = dot(placed, pe_perm[...]).astype(BF16)

    @pl.when(me < n - 1)
    def _():
        carry.wait_send()


def per_device(n, frames, clip_lengths, slot_map, stem, time, gain, mid, lat, pe):
    nframes, cin, pos = frames.shape
    c1, c2, latc = stem.shape[0], mid.shape[0], lat.shape[0]
    blocks = mid.shape[1] // c1
    cells = pos // blocks
    side = int(round(cells**0.5))
    rows = slot_map.shape[0]
    features, wide = pe.shape
    width = 2 * features
    cap = -(-max(2, 2 * rows // n) // 8) * 8
    vmem = pltpu.VMEM
    anywhere = pl.BlockSpec(memory_space=pl.ANY)
    kspan = (SPAN + 2) * cin
    return pl.pallas_call(
        functools.partial(kernel, n, side),
        out_shape=jax.ShapeDtypeStruct((rows, wide), BF16),
        in_specs=[pl.BlockSpec(memory_space=pltpu.SMEM)] + [anywhere] * 8,
        out_specs=pl.BlockSpec(memory_space=vmem),
        scratch_shapes=[
            vmem((1, rows), I32),
            vmem((1, c1), F32),
            vmem((nframes + 2, cin, pos), BF16),
            vmem(stem.shape, BF16),
            vmem(time.shape, BF16),
            vmem(mid.shape, BF16),
            vmem((nframes, latc, c2), BF16),
            vmem(pe.shape, BF16),
            vmem((SPAN * c1, kspan), BF16),
            vmem((SPAN * c1, kspan), BF16),
            vmem((c1, cells), F32),
            vmem(mid.shape, BF16),
            vmem((width, wide), BF16),
            vmem((n * cap, rows), BF16),
            vmem((SPAN, c1 // 16, blocks, 16, cells), BF16),
            vmem((n, cap, width), F32),
            vmem((n, cap, width), F32),
            pltpu.SemaphoreType.DMA((8 + nframes,)),
            pltpu.SemaphoreType.DMA((2,)),
            pltpu.SemaphoreType.DMA((n,)),
            pltpu.SemaphoreType.DMA((n,)),
        ],
        compiler_params=pltpu.CompilerParams(
            collective_id=0, has_side_effects=True, vmem_limit_bytes=56 * 2**20
        ),
        cost_estimate=pl.CostEstimate(
            flops=2 * nframes * (pos * c1 * 3 * cin + cells * c2 * c1 * blocks),
            bytes_accessed=2 * (nframes * cin * pos + mid.size + pe.size + rows * wide),
            transcendentals=nframes * pos * c1,
        ),
    )(clip_lengths, slot_map.reshape(1, rows), gain.reshape(1, c1), frames, stem, time, mid, lat, pe)


def solution(mesh):
    sharded = P(("grp", "tok"), None, None)
    return jax.shard_map(
        functools.partial(per_device, mesh.shape["tok"]),
        mesh=mesh,
        in_specs=(sharded, P("grp"), P(("grp", "tok")), P(), P(), P(), P(), P(), P()),
        out_specs=P(("grp", "tok"), None),
        check_vma=False,
    )
```

```python
import functools

import jax
import jax.numpy as jnp
from jax import lax
from jax.experimental import pallas as pl
from jax.experimental.pallas import tpu as pltpu
from jax.sharding import PartitionSpec as P

F32 = jnp.float32
BF16 = jnp.bfloat16
I32 = jnp.int32
SPAN = 2


def iota(shape, dim):
    return lax.broadcasted_iota(I32, shape, dim)


def dot(a, b, contract=((1,), (0,))):
    return lax.dot_general(a, b, (contract, ((), ())), preferred_element_type=F32)


def shift_of(size):
    assert size & (size - 1) == 0
    return size.bit_length() - 1


def kernel(
    n, side, clip_ref, slot_hbm, gain_hbm, frames_hbm, stem_hbm, time_hbm, mid_hbm, lat_hbm,
    out_ref,
    slot, gain, frames, stem, time, mid, lat,
    toeplitz, masked, wide_gain, swap, mid_perm, lat_rep, pick, select, s_ref, m_ref, outbuf, inbuf,
    load_sem, carry_send, carry_recv, send_sem, recv_sem,
):
    me = lax.axis_index("tok")
    nframes, cin, pos = frames_hbm.shape
    c1 = stem_hbm.shape[1]
    cells = side * side
    blocks = pos // cells
    c2 = mid_hbm.shape[0]
    latc = lat_hbm.shape[0]
    rows = slot_hbm.shape[1]
    cap = outbuf.shape[1]
    width = outbuf.shape[2]
    slots = n * cap
    quads = 4
    features = quads * latc
    tall = c2 // 2
    pieces = carry_send.shape[0]
    per_step = blocks // pieces
    groups = nframes // SPAN

    loads = [
        pltpu.make_async_copy(stem_hbm, stem, load_sem.at[0]),
        pltpu.make_async_copy(time_hbm, time, load_sem.at[1]),
        pltpu.make_async_copy(gain_hbm, gain, load_sem.at[2]),
        pltpu.make_async_copy(slot_hbm, slot, load_sem.at[3]),
        pltpu.make_async_copy(frames_hbm.at[0:4], frames.at[2:6], load_sem.at[4]),
        pltpu.make_async_copy(mid_hbm, mid, load_sem.at[5]),
        pltpu.make_async_copy(lat_hbm, lat, load_sem.at[6]),
        pltpu.make_async_copy(frames_hbm.at[4:nframes], frames.at[6 : nframes + 2], load_sem.at[7]),
    ]
    for load in loads:
        load.start()

    barrier = pltpu.get_barrier_semaphore()

    def greet(k, _):
        pl.semaphore_signal(
            barrier, inc=1, device_id={"tok": lax.rem(me + k, n)}, device_id_type=pl.DeviceIdType.MESH
        )
        return 0

    lax.fori_loop(1, n, greet, 0)

    @pl.when(me == 0)
    def _():
        frames[0:2] = jnp.zeros_like(frames[0:2])

    bits = shift_of(blocks)
    k_in, k_out = iota(swap.shape, 0), iota(swap.shape, 1)
    moved = ((k_in >> bits) == (k_out & 15)) & ((k_in & (blocks - 1)) == (k_out >> 4))
    swap[...] = jnp.where(moved, jnp.float32(0.5), jnp.float32(0.0)).astype(BF16)
    half = side // 2
    half_bits = shift_of(half)
    cell, row_id = iota((cells, rows), 0), iota((cells, rows), 1)
    for q in range(quads):
        a, b = q // 2, q % 2
        pick[q] = (cell == (2 * (row_id >> half_bits) + a) * side + 2 * (row_id & (half - 1)) + b).astype(BF16)

    pl.semaphore_wait(barrier, n - 1)

    wide_piece = pos // pieces

    def carry(p):
        at = pl.ds(pl.multiple_of(p * wide_piece, wide_piece), wide_piece)
        return pltpu.make_async_remote_copy(
            src_ref=frames_hbm.at[nframes - 2 : nframes, :, at],
            dst_ref=frames.at[0:2, :, at],
            send_sem=carry_send.at[p],
            recv_sem=carry_recv.at[p],
            device_id={"tok": lax.rem(me + 1, n)},
            device_id_type=pl.DeviceIdType.MESH,
        )

    @pl.when(me < n - 1)
    def _():
        for p in range(pieces):
            carry(p).start()

    start = jnp.int32(0)
    end = jnp.int32(0)
    live = jnp.int32(0)
    keep = jnp.float32(1.0)
    for c in range(clip_ref.shape[0]):
        length = clip_ref[c]
        start = end
        end = end + lax.div(length + (nframes - 1), jnp.int32(nframes))
        inside = jnp.logical_and(start <= me, me < end)
        live = jnp.where(inside, jnp.clip(length - nframes * (me - start), 0, nframes), live)
        keep = jnp.where(jnp.logical_and(inside, start == me), jnp.float32(0.0), keep)

    kspan = (SPAN + 2) * cin
    loads[0].wait()
    loads[1].wait()
    placed_stem = [
        dot(stem[...], (iota((cin, kspan), 1) == iota((cin, kspan), 0) + b * cin).astype(BF16), ((0,), (0,))).astype(BF16)
        for b in range(SPAN + 2)
    ]
    for j in range(SPAN):
        row = dot(time[2], placed_stem[j]) + dot(time[1], placed_stem[j + 1]) + dot(time[0], placed_stem[j + 2])
        toeplitz[j * c1 : (j + 1) * c1, :] = row
    column_id = iota((1, kspan), 1)
    for g in range(groups):
        first = (SPAN * (g + 1)) % nframes
        on = jnp.where(column_id < cin * (live - first + 2), jnp.float32(1.0), jnp.float32(0.0))
        on = jnp.where(column_id < cin * (2 - first), keep, on)
        masked[g] = (toeplitz[...] * on).astype(BF16)

    loads[2].wait()
    diagonal = iota((c1, c1), 0) == iota((c1, c1), 1)
    column = jnp.sum(jnp.where(diagonal, jnp.broadcast_to(gain[...], (c1, c1)), 0.0), axis=1, keepdims=True)
    wide_gain[...] = jnp.broadcast_to(0.5 * column, wide_gain.shape)

    loads[3].wait()
    row_bits = shift_of(rows)
    where_to = slot[...]
    target = where_to >> row_bits
    place = where_to & (rows - 1)
    onehot = iota((n, rows), 0) == target
    before = (iota((rows, rows), 0) < iota((rows, rows), 1)).astype(BF16)
    earlier = dot(onehot.astype(BF16), before)
    rank = jnp.sum(jnp.where(onehot, earlier, 0.0), axis=0, keepdims=True).astype(I32)
    select[...] = (iota((slots, rows), 0) == target * cap + rank).astype(BF16)

    m_ref[...] = jnp.zeros_like(m_ref)

    def conv(g, t):
        first = lax.rem(SPAN * (g + 1), nframes)
        weight = masked[g]
        for i in range(per_step):
            ab = t * per_step + i
            at = pl.ds(pl.multiple_of(ab * cells, cells), cells)
            data = frames[pl.ds(first, SPAN + 2), :, at].reshape(kspan, cells)
            h = dot(weight, data)
            for j in range(SPAN):
                hj = h[j * c1 : (j + 1) * c1]
                scale = lax.rsqrt(jnp.sum(hj * hj, axis=0, keepdims=True) * (1.0 / c1) + 1e-6)
                x = hj * scale * wide_gain[...]
                u = x + x * jnp.tanh(x)
                s_ref[first + j, :, ab] = u.astype(BF16).reshape(c1 // 16, 16, cells)

    def frame_of(unit):
        return lax.rem(SPAN + (unit >> 1), nframes)

    def gather_latent(unit, acc):
        at = frame_of(unit) * c2 + (unit & 1) * tall
        return acc + dot(lat_rep[:, pl.ds(pl.multiple_of(at, tall), tall)], m_ref[unit & 1])

    def deep(unit, acc):
        g = dot(mid_perm[unit & 1], s_ref[frame_of(unit)].reshape(c1 * blocks, cells))
        m_ref[unit & 1] = (g + g * jnp.tanh(g)).astype(BF16)
        return acc

    chunk = swap.shape[0]
    per_chunk = (c1 // 16) // pieces

    def opening(t, _):
        conv(0, t)
        for i in range(per_chunk):
            at = pl.ds(pl.multiple_of((t * per_chunk + i) * chunk, chunk), chunk)
            for top in range(2):
                mid_perm[top, :, at] = dot(mid[top * tall : (top + 1) * tall, at], swap[...]).astype(BF16)
        return 0

    loads[4].wait()
    loads[5].wait()
    lax.fori_loop(0, pieces, opening, 0)

    loads[6].wait()
    repeat = (iota((features, latc), 0) >> shift_of(quads) == iota((features, latc), 1)).astype(BF16)
    lat_rep[...] = dot(repeat, lat[...]).astype(BF16)
    loads[7].wait()

    step_bits = shift_of(pieces)

    def both(t, acc):
        acc = gather_latent(jnp.maximum(t - 1, 0), acc)
        conv(1 + (t >> step_bits), t & (pieces - 1))
        return deep(t, acc)

    middle = (groups - 2) * pieces
    acc = lax.fori_loop(0, middle, both, jnp.zeros((features, cells), F32))

    def with_carry(t, acc):
        @pl.when(me > 0)
        def _():
            carry(t).wait_recv()

        acc = gather_latent(middle + t - 1, acc)
        conv(groups - 1, t)
        return deep(middle + t, acc)

    acc = lax.fori_loop(0, pieces, with_carry, acc)

    def closing(t, acc):
        acc = gather_latent(middle + pieces + t - 1, acc)
        return deep(middle + pieces + t, acc)

    acc = lax.fori_loop(0, 2 * SPAN, closing, acc)
    latent = gather_latent(jnp.int32(2 * nframes - 1), acc).astype(BF16)

    quad = iota((features, rows), 0) & (quads - 1)
    picked = jnp.zeros((features, rows), F32)
    for q in range(quads):
        picked = jnp.where(quad == q, dot(latent, pick[q]), picked)
    tag = jnp.where(iota((width - features, rows), 0) == 0, (place + 1).astype(F32), 0.0)
    rows_t = jnp.concatenate([picked, tag], axis=0).astype(BF16)
    payload = dot(select[...], rows_t, ((1,), (1,)))
    outbuf[...] = payload.reshape(n, cap, width)

    def exchange(k):
        to = lax.rem(me + k, n)
        return pltpu.make_async_remote_copy(
            src_ref=outbuf.at[to],
            dst_ref=inbuf.at[me],
            send_sem=send_sem.at[k],
            recv_sem=recv_sem.at[k],
            device_id={"tok": to},
            device_id_type=pl.DeviceIdType.MESH,
        )

    def send(k, _):
        exchange(k).start()
        return 0

    def finish(k, _):
        exchange(k).wait()
        return 0

    lax.fori_loop(1, n, send, 0)
    inbuf[me] = outbuf[me]
    lax.fori_loop(1, n, finish, 0)

    arrived = inbuf[...].reshape(slots, width)
    arrange = (arrived[:, features : features + 1] == (iota((slots, rows), 1) + 1).astype(F32)).astype(BF16)
    placed = dot(arrange, arrived.astype(BF16), ((0,), (0,)))
    out_ref[...] = placed[:, 0:features].astype(BF16)

    @pl.when(me < n - 1)
    def _():
        for p in range(pieces):
            carry(p).wait_send()


def per_device(n, frames, clip_lengths, slot_map, stem, time, gain, mid, lat, pe):
    nframes, cin, pos = frames.shape
    c1, c2, latc = stem.shape[0], mid.shape[0], lat.shape[0]
    blocks = mid.shape[1] // c1
    cells = pos // blocks
    side = int(round(cells**0.5))
    rows = slot_map.shape[0]
    features = pe.shape[0]
    width = 2 * features
    pieces = 4
    cap = -(-max(2, 2 * rows // n) // 8) * 8
    vmem = pltpu.VMEM
    anywhere = pl.BlockSpec(memory_space=pl.ANY)
    kspan = (SPAN + 2) * cin
    placed = pl.pallas_call(
        functools.partial(kernel, n, side),
        out_shape=jax.ShapeDtypeStruct((rows, features), BF16),
        in_specs=[pl.BlockSpec(memory_space=pltpu.SMEM)] + [anywhere] * 7,
        out_specs=pl.BlockSpec(memory_space=vmem),
        scratch_shapes=[
            vmem((1, rows), I32),
            vmem((1, c1), F32),
            vmem((nframes + 2, cin, pos), BF16),
            vmem((cin, c1), BF16),
            vmem(time.shape, BF16),
            vmem(mid.shape, BF16),
            vmem(lat.shape, BF16),
            vmem((SPAN * c1, kspan), F32),
            vmem((nframes // SPAN, SPAN * c1, kspan), BF16),
            vmem((c1, cells), F32),
            vmem((16 * blocks, 16 * blocks), BF16),
            vmem((2, c2 // 2, mid.shape[1]), BF16),
            vmem((features, lat.shape[1]), BF16),
            vmem((4, cells, rows), BF16),
            vmem((n * cap, rows), BF16),
            vmem((nframes, c1 // 16, blocks, 16, cells), BF16),
            vmem((2, c2 // 2, cells), BF16),
            vmem((n, cap, width), F32),
            vmem((n, cap, width), F32),
            pltpu.SemaphoreType.DMA((8,)),
            pltpu.SemaphoreType.DMA((pieces,)),
            pltpu.SemaphoreType.DMA((pieces,)),
            pltpu.SemaphoreType.DMA((n,)),
            pltpu.SemaphoreType.DMA((n,)),
        ],
        compiler_params=pltpu.CompilerParams(
            collective_id=0, has_side_effects=True, vmem_limit_bytes=56 * 2**20
        ),
        cost_estimate=pl.CostEstimate(
            flops=2 * nframes * (pos * c1 * 3 * cin + cells * c2 * c1 * blocks),
            bytes_accessed=2 * (nframes * cin * pos + mid.size + rows * features),
            transcendentals=nframes * pos * c1,
        ),
    )(clip_lengths, slot_map.reshape(1, rows), gain.reshape(1, c1), frames, stem.T, time, mid, lat)
    return jnp.dot(placed, pe, preferred_element_type=F32).astype(BF16)


def solution(mesh):
    sharded = P(("grp", "tok"), None, None)
    return jax.shard_map(
        functools.partial(per_device, mesh.shape["tok"]),
        mesh=mesh,
        in_specs=(sharded, P("grp"), P(("grp", "tok")), P(), P(), P(), P(), P(), P()),
        out_specs=P(("grp", "tok"), None),
        check_vma=False,
    )
```

```python
import functools

import jax
import jax.numpy as jnp
from jax import lax
from jax.experimental import pallas as pl
from jax.experimental.pallas import tpu as pltpu
from jax.sharding import PartitionSpec as P

F32 = jnp.float32
BF16 = jnp.bfloat16
I32 = jnp.int32
SPAN = 2


def iota(shape, dim):
    return lax.broadcasted_iota(I32, shape, dim)


def dot(a, b, contract=((1,), (0,))):
    return lax.dot_general(a, b, (contract, ((), ())), preferred_element_type=F32)


def shift_of(size):
    assert size & (size - 1) == 0
    return size.bit_length() - 1


def kernel(
    n, side, clip_ref, slot_hbm, gain_hbm, frames_hbm, stem_hbm, time_hbm, mid_hbm, lat_hbm,
    out_ref,
    slot, gain, frames, stem, time, mid, lat,
    toeplitz, masked, wide_gain, swap, mid_perm, lat_rep, pick, select, s_ref, m_ref, outbuf, inbuf,
    load_sem, carry_send, carry_recv, send_sem, recv_sem,
):
    me = lax.axis_index("tok")
    nframes, cin, pos = frames_hbm.shape
    c1 = stem_hbm.shape[1]
    cells = side * side
    blocks = pos // cells
    c2 = mid_hbm.shape[0]
    latc = lat_hbm.shape[0]
    rows = slot_hbm.shape[1]
    cap = outbuf.shape[1]
    width = outbuf.shape[2]
    slots = n * cap
    quads = 4
    features = quads * latc
    tall = c2 // 2
    pieces = carry_send.shape[0]
    per_step = blocks // pieces
    groups = nframes // SPAN

    loads = [
        pltpu.make_async_copy(stem_hbm, stem, load_sem.at[0]),
        pltpu.make_async_copy(time_hbm, time, load_sem.at[1]),
        pltpu.make_async_copy(gain_hbm, gain, load_sem.at[2]),
        pltpu.make_async_copy(slot_hbm, slot, load_sem.at[3]),
        pltpu.make_async_copy(frames_hbm.at[0:4], frames.at[2:6], load_sem.at[4]),
        pltpu.make_async_copy(mid_hbm, mid, load_sem.at[5]),
        pltpu.make_async_copy(lat_hbm, lat, load_sem.at[6]),
        pltpu.make_async_copy(frames_hbm.at[4:nframes], frames.at[6 : nframes + 2], load_sem.at[7]),
    ]
    for load in loads:
        load.start()

    barrier = pltpu.get_barrier_semaphore()

    def greet(k, _):
        pl.semaphore_signal(
            barrier, inc=1, device_id={"tok": lax.rem(me + k, n)}, device_id_type=pl.DeviceIdType.MESH
        )
        return 0

    lax.fori_loop(1, n, greet, 0)

    @pl.when(me == 0)
    def _():
        frames[0:2] = jnp.zeros_like(frames[0:2])

    bits = shift_of(blocks)
    k_in, k_out = iota(swap.shape, 0), iota(swap.shape, 1)
    moved = ((k_in >> bits) == (k_out & 15)) & ((k_in & (blocks - 1)) == (k_out >> 4))
    swap[...] = jnp.where(moved, jnp.float32(0.5), jnp.float32(0.0)).astype(BF16)
    half = side // 2
    half_bits = shift_of(half)
    cell, row_id = iota((cells, rows), 0), iota((cells, rows), 1)
    for q in range(quads):
        a, b = q // 2, q % 2
        pick[q] = (cell == (2 * (row_id >> half_bits) + a) * side + 2 * (row_id & (half - 1)) + b).astype(BF16)

    pl.semaphore_wait(barrier, n - 1)

    wide_piece = pos // pieces

    def carry(p):
        at = pl.ds(pl.multiple_of(p * wide_piece, wide_piece), wide_piece)
        return pltpu.make_async_remote_copy(
            src_ref=frames_hbm.at[nframes - 2 : nframes, :, at],
            dst_ref=frames.at[0:2, :, at],
            send_sem=carry_send.at[p],
            recv_sem=carry_recv.at[p],
            device_id={"tok": lax.rem(me + 1, n)},
            device_id_type=pl.DeviceIdType.MESH,
        )

    @pl.when(me < n - 1)
    def _():
        for p in range(pieces):
            carry(p).start()

    start = jnp.int32(0)
    end = jnp.int32(0)
    live = jnp.int32(0)
    keep = jnp.float32(1.0)
    for c in range(clip_ref.shape[0]):
        length = clip_ref[c]
        start = end
        end = end + lax.div(length + (nframes - 1), jnp.int32(nframes))
        inside = jnp.logical_and(start <= me, me < end)
        live = jnp.where(inside, jnp.clip(length - nframes * (me - start), 0, nframes), live)
        keep = jnp.where(jnp.logical_and(inside, start == me), jnp.float32(0.0), keep)

    kspan = (SPAN + 2) * cin
    loads[0].wait()
    loads[1].wait()
    placed_stem = [
        dot(stem[...], (iota((cin, kspan), 1) == iota((cin, kspan), 0) + b * cin).astype(BF16), ((0,), (0,))).astype(BF16)
        for b in range(SPAN + 2)
    ]
    for j in range(SPAN):
        row = dot(time[2], placed_stem[j]) + dot(time[1], placed_stem[j + 1]) + dot(time[0], placed_stem[j + 2])
        toeplitz[j * c1 : (j + 1) * c1, :] = row
    column_id = iota((1, kspan), 1)
    for g in range(groups):
        first = (SPAN * (g + 1)) % nframes
        on = jnp.where(column_id < cin * (live - first + 2), jnp.float32(1.0), jnp.float32(0.0))
        on = jnp.where(column_id < cin * (2 - first), keep, on)
        masked[g] = (toeplitz[...] * on).astype(BF16)

    loads[2].wait()
    diagonal = iota((c1, c1), 0) == iota((c1, c1), 1)
    column = jnp.sum(jnp.where(diagonal, jnp.broadcast_to(gain[...], (c1, c1)), 0.0), axis=1, keepdims=True)
    wide_gain[...] = jnp.broadcast_to(0.5 * column, wide_gain.shape)

    loads[3].wait()
    row_bits = shift_of(rows)
    where_to = slot[...]
    target = where_to >> row_bits
    place = where_to & (rows - 1)
    onehot = iota((n, rows), 0) == target
    before = (iota((rows, rows), 0) < iota((rows, rows), 1)).astype(BF16)
    earlier = dot(onehot.astype(BF16), before)
    rank = jnp.sum(jnp.where(onehot, earlier, 0.0), axis=0, keepdims=True).astype(I32)
    select[...] = (iota((slots, rows), 0) == target * cap + rank).astype(BF16)

    m_ref[...] = jnp.zeros_like(m_ref)

    def conv(g, t):
        first = lax.rem(SPAN * (g + 1), nframes)
        weight = masked[g]
        for i in range(per_step):
            ab = t * per_step + i
            at = pl.ds(pl.multiple_of(ab * cells, cells), cells)
            data = frames[pl.ds(first, SPAN + 2), :, at].reshape(kspan, cells)
            h = dot(weight, data)
            for j in range(SPAN):
                for lane in range(0, cells, 128):
                    hj = h[j * c1 : (j + 1) * c1, lane : lane + 128]
                    scale = lax.rsqrt(jnp.sum(hj * hj, axis=0, keepdims=True) * (1.0 / c1) + 1e-6)
                    for q in range(c1 // 16):
                        x = hj[q * 16 : (q + 1) * 16] * scale * wide_gain[q * 16 : (q + 1) * 16, :]
                        u = x + x * jnp.tanh(x)
                        s_ref[first + j, q, ab, :, lane : lane + 128] = u.astype(BF16)

    def frame_of(unit):
        return lax.rem(SPAN + (unit >> 1), nframes)

    def gather_latent(unit, acc):
        at = frame_of(unit) * c2 + (unit & 1) * tall
        return acc + dot(lat_rep[:, pl.ds(pl.multiple_of(at, tall), tall)], m_ref[unit & 1])

    def deep(unit, acc):
        g = dot(mid_perm[unit & 1], s_ref[frame_of(unit)].reshape(c1 * blocks, cells))
        for q in range(0, tall, 32):
            part = g[q : q + 32]
            m_ref[unit & 1, q : q + 32, :] = (part + part * jnp.tanh(part)).astype(BF16)
        return acc

    chunk = swap.shape[0]
    per_chunk = (c1 // 16) // pieces

    def opening(t, _):
        conv(0, t)
        for i in range(per_chunk):
            at = pl.ds(pl.multiple_of((t * per_chunk + i) * chunk, chunk), chunk)
            for top in range(2):
                mid_perm[top, :, at] = dot(mid[top * tall : (top + 1) * tall, at], swap[...]).astype(BF16)
        return 0

    loads[4].wait()
    loads[5].wait()
    lax.fori_loop(0, pieces, opening, 0)

    loads[6].wait()
    repeat = (iota((features, latc), 0) >> shift_of(quads) == iota((features, latc), 1)).astype(BF16)
    lat_rep[...] = dot(repeat, lat[...]).astype(BF16)
    loads[7].wait()

    step_bits = shift_of(pieces)

    def both(t, acc):
        acc = gather_latent(jnp.maximum(t - 1, 0), acc)
        conv(1 + (t >> step_bits), t & (pieces - 1))
        return deep(t, acc)

    middle = (groups - 2) * pieces
    acc = lax.fori_loop(0, middle, both, jnp.zeros((features, cells), F32))

    def with_carry(t, acc):
        @pl.when(me > 0)
        def _():
            carry(t).wait_recv()

        acc = gather_latent(middle + t - 1, acc)
        conv(groups - 1, t)
        return deep(middle + t, acc)

    acc = lax.fori_loop(0, pieces, with_carry, acc)

    def closing(t, acc):
        acc = gather_latent(middle + pieces + t - 1, acc)
        return deep(middle + pieces + t, acc)

    acc = lax.fori_loop(0, 2 * SPAN, closing, acc)
    latent = gather_latent(jnp.int32(2 * nframes - 1), acc).astype(BF16)

    quad = iota((features, rows), 0) & (quads - 1)
    picked = jnp.zeros((features, rows), F32)
    for q in range(quads):
        picked = jnp.where(quad == q, dot(latent, pick[q]), picked)
    tag = jnp.where(iota((width - features, rows), 0) == 0, (place + 1).astype(F32), 0.0)
    rows_t = jnp.concatenate([picked, tag], axis=0).astype(BF16)
    payload = dot(select[...], rows_t, ((1,), (1,)))
    outbuf[...] = payload.reshape(n, cap, width)

    def exchange(k):
        to = lax.rem(me + k, n)
        return pltpu.make_async_remote_copy(
            src_ref=outbuf.at[to],
            dst_ref=inbuf.at[me],
            send_sem=send_sem.at[k],
            recv_sem=recv_sem.at[k],
            device_id={"tok": to},
            device_id_type=pl.DeviceIdType.MESH,
        )

    def send(k, _):
        exchange(k).start()
        return 0

    def finish(k, _):
        exchange(k).wait()
        return 0

    lax.fori_loop(1, n, send, 0)
    inbuf[me] = outbuf[me]
    lax.fori_loop(1, n, finish, 0)

    arrived = inbuf[...].reshape(slots, width)
    arrange = (arrived[:, features : features + 1] == (iota((slots, rows), 1) + 1).astype(F32)).astype(BF16)
    placed = dot(arrange, arrived.astype(BF16), ((0,), (0,)))
    out_ref[...] = placed[:, 0:features].astype(BF16)

    @pl.when(me < n - 1)
    def _():
        for p in range(pieces):
            carry(p).wait_send()


def per_device(n, frames, clip_lengths, slot_map, stem, time, gain, mid, lat, pe):
    nframes, cin, pos = frames.shape
    c1, c2, latc = stem.shape[0], mid.shape[0], lat.shape[0]
    blocks = mid.shape[1] // c1
    cells = pos // blocks
    side = int(round(cells**0.5))
    rows = slot_map.shape[0]
    features = pe.shape[0]
    width = 2 * features
    pieces = 4
    cap = -(-max(2, 2 * rows // n) // 8) * 8
    vmem = pltpu.VMEM
    anywhere = pl.BlockSpec(memory_space=pl.ANY)
    kspan = (SPAN + 2) * cin
    placed = pl.pallas_call(
        functools.partial(kernel, n, side),
        out_shape=jax.ShapeDtypeStruct((rows, features), BF16),
        in_specs=[pl.BlockSpec(memory_space=pltpu.SMEM)] + [anywhere] * 7,
        out_specs=pl.BlockSpec(memory_space=vmem),
        scratch_shapes=[
            vmem((1, rows), I32),
            vmem((1, c1), F32),
            vmem((nframes + 2, cin, pos), BF16),
            vmem((cin, c1), BF16),
            vmem(time.shape, BF16),
            vmem(mid.shape, BF16),
            vmem(lat.shape, BF16),
            vmem((SPAN * c1, kspan), F32),
            vmem((nframes // SPAN, SPAN * c1, kspan), BF16),
            vmem((c1, 128), F32),
            vmem((16 * blocks, 16 * blocks), BF16),
            vmem((2, c2 // 2, mid.shape[1]), BF16),
            vmem((features, lat.shape[1]), BF16),
            vmem((4, cells, rows), BF16),
            vmem((n * cap, rows), BF16),
            vmem((nframes, c1 // 16, blocks, 16, cells), BF16),
            vmem((2, c2 // 2, cells), BF16),
            vmem((n, cap, width), F32),
            vmem((n, cap, width), F32),
            pltpu.SemaphoreType.DMA((8,)),
            pltpu.SemaphoreType.DMA((pieces,)),
            pltpu.SemaphoreType.DMA((pieces,)),
            pltpu.SemaphoreType.DMA((n,)),
            pltpu.SemaphoreType.DMA((n,)),
        ],
        compiler_params=pltpu.CompilerParams(
            collective_id=0, has_side_effects=True, vmem_limit_bytes=56 * 2**20
        ),
        cost_estimate=pl.CostEstimate(
            flops=2 * nframes * (pos * c1 * 3 * cin + cells * c2 * c1 * blocks),
            bytes_accessed=2 * (nframes * cin * pos + mid.size + rows * features),
            transcendentals=nframes * pos * c1,
        ),
    )(clip_lengths, slot_map.reshape(1, rows), gain.reshape(1, c1), frames, stem.T, time, mid, lat)
    return jnp.dot(placed, pe, preferred_element_type=F32).astype(BF16)


def solution(mesh):
    sharded = P(("grp", "tok"), None, None)
    return jax.shard_map(
        functools.partial(per_device, mesh.shape["tok"]),
        mesh=mesh,
        in_specs=(sharded, P("grp"), P(("grp", "tok")), P(), P(), P(), P(), P(), P()),
        out_specs=P(("grp", "tok"), None),
        check_vma=False,
    )
```

```python
import functools

import jax
import jax.numpy as jnp
from jax import lax
from jax.experimental import pallas as pl
from jax.experimental.pallas import tpu as pltpu
from jax.sharding import PartitionSpec as P

F32 = jnp.float32
BF16 = jnp.bfloat16
I32 = jnp.int32
SPAN = 2


def iota(shape, dim):
    return lax.broadcasted_iota(I32, shape, dim)


def dot(a, b, contract=((1,), (0,))):
    return lax.dot_general(a, b, (contract, ((), ())), preferred_element_type=F32)


def wrap(index, size):
    return jnp.where(index >= size, index - size, index)


def shift_of(size):
    assert size & (size - 1) == 0
    return size.bit_length() - 1


def kernel(
    n, side, clip_ref, slot_hbm, gain_hbm, frames_hbm, stem_hbm, time_hbm, mid_hbm, lat_hbm,
    out_ref,
    slot, gain, frames, stem, time, mid, lat,
    toeplitz, masked, wide_gain, swap, mid_perm, lat_rep, pick, select, s_ref, m_ref, outbuf, inbuf,
    load_sem, carry_send, carry_recv, send_sem, recv_sem,
):
    me = lax.axis_index("tok")
    nframes, cin, pos = frames_hbm.shape
    c1 = stem_hbm.shape[1]
    cells = side * side
    blocks = pos // cells
    c2 = mid_hbm.shape[0]
    latc = lat_hbm.shape[0]
    rows = slot_hbm.shape[1]
    cap = outbuf.shape[1]
    width = outbuf.shape[2]
    slots = n * cap
    quads = 4
    features = quads * latc
    pieces = carry_send.shape[0]
    steps = 2
    per_step = blocks // steps
    groups = nframes // SPAN

    loads = [
        pltpu.make_async_copy(stem_hbm, stem, load_sem.at[0]),
        pltpu.make_async_copy(time_hbm, time, load_sem.at[1]),
        pltpu.make_async_copy(gain_hbm, gain, load_sem.at[2]),
        pltpu.make_async_copy(slot_hbm, slot, load_sem.at[3]),
        pltpu.make_async_copy(frames_hbm.at[0:4], frames.at[2:6], load_sem.at[4]),
        pltpu.make_async_copy(mid_hbm, mid, load_sem.at[5]),
        pltpu.make_async_copy(lat_hbm, lat, load_sem.at[6]),
        pltpu.make_async_copy(frames_hbm.at[4:nframes], frames.at[6 : nframes + 2], load_sem.at[7]),
    ]
    for load in loads:
        load.start()

    barrier = pltpu.get_barrier_semaphore()

    def greet(k, _):
        pl.semaphore_signal(
            barrier, inc=1, device_id={"tok": wrap(me + k, n)}, device_id_type=pl.DeviceIdType.MESH
        )
        return 0

    lax.fori_loop(1, n, greet, 0)

    @pl.when(me == 0)
    def _():
        frames[0:2] = jnp.zeros_like(frames[0:2])

    bits = shift_of(blocks)
    k_in, k_out = iota(swap.shape, 0), iota(swap.shape, 1)
    moved = ((k_in >> bits) == (k_out & 15)) & ((k_in & (blocks - 1)) == (k_out >> 4))
    swap[...] = jnp.where(moved, jnp.float32(0.5), jnp.float32(0.0)).astype(BF16)
    half = side // 2
    half_bits = shift_of(half)
    cell, row_id = iota((cells, rows), 0), iota((cells, rows), 1)
    for q in range(quads):
        a, b = q // 2, q % 2
        pick[q] = (cell == (2 * (row_id >> half_bits) + a) * side + 2 * (row_id & (half - 1)) + b).astype(BF16)

    pl.semaphore_wait(barrier, n - 1)

    wide_piece = pos // pieces

    def carry(p):
        at = pl.ds(pl.multiple_of(p * wide_piece, wide_piece), wide_piece)
        return pltpu.make_async_remote_copy(
            src_ref=frames_hbm.at[nframes - 2 : nframes, :, at],
            dst_ref=frames.at[0:2, :, at],
            send_sem=carry_send.at[p],
            recv_sem=carry_recv.at[p],
            device_id={"tok": wrap(me + 1, n)},
            device_id_type=pl.DeviceIdType.MESH,
        )

    @pl.when(me < n - 1)
    def _():
        for p in range(pieces):
            carry(p).start()

    start = jnp.int32(0)
    end = jnp.int32(0)
    live = jnp.int32(0)
    keep = jnp.float32(1.0)
    for c in range(clip_ref.shape[0]):
        length = clip_ref[c]
        start = end
        end = end + ((length + (nframes - 1)) >> shift_of(nframes))
        inside = jnp.logical_and(start <= me, me < end)
        live = jnp.where(inside, jnp.clip(length - nframes * (me - start), 0, nframes), live)
        keep = jnp.where(jnp.logical_and(inside, start == me), jnp.float32(0.0), keep)

    kspan = (SPAN + 2) * cin
    loads[0].wait()
    loads[1].wait()
    placed_stem = [
        dot(stem[...], (iota((cin, kspan), 1) == iota((cin, kspan), 0) + b * cin).astype(BF16), ((0,), (0,))).astype(BF16)
        for b in range(SPAN + 2)
    ]
    for j in range(SPAN):
        row = dot(time[2], placed_stem[j]) + dot(time[1], placed_stem[j + 1]) + dot(time[0], placed_stem[j + 2])
        toeplitz[j * c1 : (j + 1) * c1, :] = row
    column_id = iota((1, kspan), 1)
    for g in range(groups):
        first = (SPAN * (g + 1)) % nframes
        on = jnp.where(column_id < cin * (live - first + 2), jnp.float32(1.0), jnp.float32(0.0))
        on = jnp.where(column_id < cin * (2 - first), keep, on)
        masked[g] = (toeplitz[...] * on).astype(BF16)

    loads[2].wait()
    diagonal = iota((c1, c1), 0) == iota((c1, c1), 1)
    column = jnp.sum(jnp.where(diagonal, jnp.broadcast_to(gain[...], (c1, c1)), 0.0), axis=1, keepdims=True)
    wide_gain[...] = jnp.broadcast_to(0.5 * column, wide_gain.shape)

    loads[3].wait()
    row_bits = shift_of(rows)
    where_to = slot[...]
    target = where_to >> row_bits
    place = where_to & (rows - 1)
    onehot = iota((n, rows), 0) == target
    before = (iota((rows, rows), 0) < iota((rows, rows), 1)).astype(BF16)
    earlier = dot(onehot.astype(BF16), before)
    rank = jnp.sum(jnp.where(onehot, earlier, 0.0), axis=0, keepdims=True).astype(I32)
    select[...] = (iota((slots, rows), 0) == target * cap + rank).astype(BF16)

    m_ref[...] = jnp.zeros_like(m_ref)

    def conv(g, t):
        first = (SPAN * (g + 1)) & (nframes - 1)
        weight = masked[g]
        for i in range(per_step):
            ab = t * per_step + i
            at = pl.ds(pl.multiple_of(ab * cells, cells), cells)
            data = frames[pl.ds(first, SPAN + 2), :, at].reshape(kspan, cells)
            h = dot(weight, data)
            for j in range(SPAN):
                for lane in range(0, cells, 128):
                    hj = h[j * c1 : (j + 1) * c1, lane : lane + 128]
                    scale = lax.rsqrt(jnp.sum(hj * hj, axis=0, keepdims=True) * (1.0 / c1) + 1e-6)
                    for q in range(c1 // 16):
                        x = hj[q * 16 : (q + 1) * 16] * scale * wide_gain[q * 16 : (q + 1) * 16, :]
                        u = x + x * jnp.tanh(x)
                        s_ref[first + j, q, ab, :, lane : lane + 128] = u.astype(BF16)

    def frame_of(unit):
        return (SPAN + unit) & (nframes - 1)

    def gather_latent(unit, acc):
        at = frame_of(unit) * c2
        return acc + dot(lat_rep[:, pl.ds(pl.multiple_of(at, c2), c2)], m_ref[unit & 1])

    def deep(unit, acc):
        g = dot(mid_perm[...], s_ref[frame_of(unit)].reshape(c1 * blocks, cells))
        for q in range(0, c2, 32):
            part = g[q : q + 32]
            m_ref[unit & 1, q : q + 32, :] = (part + part * jnp.tanh(part)).astype(BF16)
        return acc

    chunk = swap.shape[0]
    per_chunk = (c1 // 16) // steps

    def opening(t, _):
        conv(0, t)
        for i in range(per_chunk):
            at = pl.ds(pl.multiple_of((t * per_chunk + i) * chunk, chunk), chunk)
            mid_perm[:, at] = dot(mid[:, at], swap[...]).astype(BF16)
        return 0

    loads[4].wait()
    loads[5].wait()
    lax.fori_loop(0, steps, opening, 0)

    loads[6].wait()
    repeat = (iota((features, latc), 0) >> shift_of(quads) == iota((features, latc), 1)).astype(BF16)
    lat_rep[...] = dot(repeat, lat[...]).astype(BF16)
    loads[7].wait()

    step_bits = shift_of(steps)

    def both(t, acc):
        acc = gather_latent(jnp.maximum(t - 1, 0), acc)
        conv(1 + (t >> step_bits), t & (steps - 1))
        return deep(t, acc)

    middle = (groups - 2) * steps
    acc = lax.fori_loop(0, middle, both, jnp.zeros((features, cells), F32))

    def with_carry(t, acc):
        @pl.when(me > 0)
        def _():
            for p in range(pieces // steps):
                carry(t * (pieces // steps) + p).wait_recv()

        acc = gather_latent(middle + t - 1, acc)
        conv(groups - 1, t)
        return deep(middle + t, acc)

    acc = lax.fori_loop(0, steps, with_carry, acc)

    def closing(t, acc):
        acc = gather_latent(middle + steps + t - 1, acc)
        return deep(middle + steps + t, acc)

    acc = lax.fori_loop(0, SPAN, closing, acc)
    latent = gather_latent(jnp.int32(nframes - 1), acc).astype(BF16)

    quad = iota((features, rows), 0) & (quads - 1)
    picked = jnp.zeros((features, rows), F32)
    for q in range(quads):
        picked = jnp.where(quad == q, dot(latent, pick[q]), picked)
    tag = jnp.where(iota((width - features, rows), 0) == 0, (place + 1).astype(F32), 0.0)
    rows_t = jnp.concatenate([picked, tag], axis=0).astype(BF16)
    payload = dot(select[...], rows_t, ((1,), (1,)))
    outbuf[...] = payload.reshape(n, cap, width)

    def exchange(k):
        to = wrap(me + k, n)
        return pltpu.make_async_remote_copy(
            src_ref=outbuf.at[to],
            dst_ref=inbuf.at[me],
            send_sem=send_sem.at[k],
            recv_sem=recv_sem.at[k],
            device_id={"tok": to},
            device_id_type=pl.DeviceIdType.MESH,
        )

    def send(k, _):
        exchange(k).start()
        return 0

    def finish(k, _):
        exchange(k).wait()
        return 0

    lax.fori_loop(1, n, send, 0)
    inbuf[me] = outbuf[me]
    lax.fori_loop(1, n, finish, 0)

    arrived = inbuf[...].reshape(slots, width)
    arrange = (arrived[:, features : features + 1] == (iota((slots, rows), 1) + 1).astype(F32)).astype(BF16)
    placed = dot(arrange, arrived.astype(BF16), ((0,), (0,)))
    out_ref[...] = placed[:, 0:features].astype(BF16)

    @pl.when(me < n - 1)
    def _():
        for p in range(pieces):
            carry(p).wait_send()


def per_device(n, frames, clip_lengths, slot_map, stem, time, gain, mid, lat, pe):
    nframes, cin, pos = frames.shape
    c1, c2, latc = stem.shape[0], mid.shape[0], lat.shape[0]
    blocks = mid.shape[1] // c1
    cells = pos // blocks
    side = int(round(cells**0.5))
    rows = slot_map.shape[0]
    features = pe.shape[0]
    width = 2 * features
    pieces = 4
    cap = -(-max(2, 2 * rows // n) // 8) * 8
    vmem = pltpu.VMEM
    anywhere = pl.BlockSpec(memory_space=pl.ANY)
    kspan = (SPAN + 2) * cin
    placed = pl.pallas_call(
        functools.partial(kernel, n, side),
        out_shape=jax.ShapeDtypeStruct((rows, features), BF16),
        in_specs=[pl.BlockSpec(memory_space=pltpu.SMEM)] + [anywhere] * 7,
        out_specs=pl.BlockSpec(memory_space=vmem),
        scratch_shapes=[
            vmem((1, rows), I32),
            vmem((1, c1), F32),
            vmem((nframes + 2, cin, pos), BF16),
            vmem((cin, c1), BF16),
            vmem(time.shape, BF16),
            vmem(mid.shape, BF16),
            vmem(lat.shape, BF16),
            vmem((SPAN * c1, kspan), F32),
            vmem((nframes // SPAN, SPAN * c1, kspan), BF16),
            vmem((c1, 128), F32),
            vmem((16 * blocks, 16 * blocks), BF16),
            vmem(mid.shape, BF16),
            vmem((features, lat.shape[1]), BF16),
            vmem((4, cells, rows), BF16),
            vmem((n * cap, rows), BF16),
            vmem((nframes, c1 // 16, blocks, 16, cells), BF16),
            vmem((2, c2, cells), BF16),
            vmem((n, cap, width), F32),
            vmem((n, cap, width), F32),
            pltpu.SemaphoreType.DMA((8,)),
            pltpu.SemaphoreType.DMA((pieces,)),
            pltpu.SemaphoreType.DMA((pieces,)),
            pltpu.SemaphoreType.DMA((n,)),
            pltpu.SemaphoreType.DMA((n,)),
        ],
        compiler_params=pltpu.CompilerParams(
            collective_id=0, has_side_effects=True, vmem_limit_bytes=56 * 2**20
        ),
        cost_estimate=pl.CostEstimate(
            flops=2 * nframes * (pos * c1 * 3 * cin + cells * c2 * c1 * blocks),
            bytes_accessed=2 * (nframes * cin * pos + mid.size + rows * features),
            transcendentals=nframes * pos * c1,
        ),
    )(clip_lengths, slot_map.reshape(1, rows), gain.reshape(1, c1), frames, stem.T, time, mid, lat)
    return jnp.dot(placed, pe, preferred_element_type=F32).astype(BF16)


def solution(mesh):
    sharded = P(("grp", "tok"), None, None)
    return jax.shard_map(
        functools.partial(per_device, mesh.shape["tok"]),
        mesh=mesh,
        in_specs=(sharded, P("grp"), P(("grp", "tok")), P(), P(), P(), P(), P(), P()),
        out_specs=P(("grp", "tok"), None),
        check_vma=False,
    )
```

```python
import functools

import jax
import jax.numpy as jnp
from jax import lax
from jax.experimental import pallas as pl
from jax.experimental.pallas import tpu as pltpu
from jax.sharding import PartitionSpec as P

F32 = jnp.float32
BF16 = jnp.bfloat16
I32 = jnp.int32
SPAN = 2


def iota(shape, dim):
    return lax.broadcasted_iota(I32, shape, dim)


def dot(a, b, contract=((1,), (0,))):
    return lax.dot_general(a, b, (contract, ((), ())), preferred_element_type=F32)


def wrap(index, size):
    return jnp.where(index >= size, index - size, index)


def shift_of(size):
    assert size & (size - 1) == 0
    return size.bit_length() - 1


def kernel(
    n, side, clip_ref, slot_hbm, gain_hbm, frames_hbm, stem_hbm, time_hbm, mid_hbm, lat_hbm,
    out_ref,
    slot, gain, frames, stem, time, mid, lat,
    toeplitz, masked, wide_gain, swap, mid_perm, lat_rep, pick, select, s_ref, m_ref, outbuf, inbuf,
    load_sem, carry_send, carry_recv, send_sem, recv_sem,
):
    me = lax.axis_index("tok")
    nframes, cin, pos = frames_hbm.shape
    c1 = stem_hbm.shape[1]
    cells = side * side
    blocks = pos // cells
    c2 = mid_hbm.shape[0]
    latc = lat_hbm.shape[0]
    rows = slot_hbm.shape[1]
    cap = outbuf.shape[1]
    width = outbuf.shape[2]
    slots = n * cap
    quads = 4
    features = quads * latc
    pieces = carry_send.shape[0]
    steps = 1
    units = SPAN // steps
    per_step = blocks // steps
    groups = nframes // SPAN

    loads = [
        pltpu.make_async_copy(stem_hbm, stem, load_sem.at[0]),
        pltpu.make_async_copy(time_hbm, time, load_sem.at[1]),
        pltpu.make_async_copy(gain_hbm, gain, load_sem.at[2]),
        pltpu.make_async_copy(slot_hbm, slot, load_sem.at[3]),
        pltpu.make_async_copy(frames_hbm.at[0:4], frames.at[2:6], load_sem.at[4]),
        pltpu.make_async_copy(mid_hbm, mid, load_sem.at[5]),
        pltpu.make_async_copy(lat_hbm, lat, load_sem.at[6]),
        pltpu.make_async_copy(frames_hbm.at[4:nframes], frames.at[6 : nframes + 2], load_sem.at[7]),
    ]
    for load in loads:
        load.start()

    barrier = pltpu.get_barrier_semaphore()

    def greet(k, _):
        pl.semaphore_signal(
            barrier, inc=1, device_id={"tok": wrap(me + k, n)}, device_id_type=pl.DeviceIdType.MESH
        )
        return 0

    lax.fori_loop(1, n, greet, 0)

    @pl.when(me == 0)
    def _():
        frames[0:2] = jnp.zeros_like(frames[0:2])

    bits = shift_of(blocks)
    k_in, k_out = iota(swap.shape, 0), iota(swap.shape, 1)
    moved = ((k_in >> bits) == (k_out & 15)) & ((k_in & (blocks - 1)) == (k_out >> 4))
    swap[...] = jnp.where(moved, jnp.float32(0.5), jnp.float32(0.0)).astype(BF16)
    half = side // 2
    half_bits = shift_of(half)
    cell, row_id = iota((cells, rows), 0), iota((cells, rows), 1)
    for q in range(quads):
        a, b = q // 2, q % 2
        pick[q] = (cell == (2 * (row_id >> half_bits) + a) * side + 2 * (row_id & (half - 1)) + b).astype(BF16)

    pl.semaphore_wait(barrier, n - 1)

    wide_piece = pos // pieces

    def carry(p):
        at = pl.ds(pl.multiple_of(p * wide_piece, wide_piece), wide_piece)
        return pltpu.make_async_remote_copy(
            src_ref=frames_hbm.at[nframes - 2 : nframes, :, at],
            dst_ref=frames.at[0:2, :, at],
            send_sem=carry_send.at[p],
            recv_sem=carry_recv.at[p],
            device_id={"tok": wrap(me + 1, n)},
            device_id_type=pl.DeviceIdType.MESH,
        )

    @pl.when(me < n - 1)
    def _():
        for p in range(pieces):
            carry(p).start()

    start = jnp.int32(0)
    end = jnp.int32(0)
    live = jnp.int32(0)
    keep = jnp.float32(1.0)
    for c in range(clip_ref.shape[0]):
        length = clip_ref[c]
        start = end
        end = end + ((length + (nframes - 1)) >> shift_of(nframes))
        inside = jnp.logical_and(start <= me, me < end)
        live = jnp.where(inside, jnp.clip(length - nframes * (me - start), 0, nframes), live)
        keep = jnp.where(jnp.logical_and(inside, start == me), jnp.float32(0.0), keep)

    kspan = (SPAN + 2) * cin
    loads[0].wait()
    loads[1].wait()
    placed_stem = [
        dot(stem[...], (iota((cin, kspan), 1) == iota((cin, kspan), 0) + b * cin).astype(BF16), ((0,), (0,))).astype(BF16)
        for b in range(SPAN + 2)
    ]
    for j in range(SPAN):
        row = dot(time[2], placed_stem[j]) + dot(time[1], placed_stem[j + 1]) + dot(time[0], placed_stem[j + 2])
        toeplitz[j * c1 : (j + 1) * c1, :] = row
    column_id = iota((1, kspan), 1)
    for g in range(groups):
        first = (SPAN * (g + 1)) % nframes
        on = jnp.where(column_id < cin * (live - first + 2), jnp.float32(1.0), jnp.float32(0.0))
        on = jnp.where(column_id < cin * (2 - first), keep, on)
        masked[g] = (toeplitz[...] * on).astype(BF16)

    loads[2].wait()
    diagonal = iota((c1, c1), 0) == iota((c1, c1), 1)
    column = jnp.sum(jnp.where(diagonal, jnp.broadcast_to(gain[...], (c1, c1)), 0.0), axis=1, keepdims=True)
    wide_gain[...] = jnp.broadcast_to(0.5 * column, wide_gain.shape)

    loads[3].wait()
    row_bits = shift_of(rows)
    where_to = slot[...]
    target = where_to >> row_bits
    place = where_to & (rows - 1)
    onehot = iota((n, rows), 0) == target
    before = (iota((rows, rows), 0) < iota((rows, rows), 1)).astype(BF16)
    earlier = dot(onehot.astype(BF16), before)
    rank = jnp.sum(jnp.where(onehot, earlier, 0.0), axis=0, keepdims=True).astype(I32)
    select[...] = (iota((slots, rows), 0) == target * cap + rank).astype(BF16)

    m_ref[...] = jnp.zeros_like(m_ref)

    def conv(g, t):
        first = (SPAN * (g + 1)) & (nframes - 1)
        weight = masked[g]
        for i in range(per_step):
            ab = t * per_step + i
            at = pl.ds(pl.multiple_of(ab * cells, cells), cells)
            data = frames[pl.ds(first, SPAN + 2), :, at].reshape(kspan, cells)
            h = dot(weight, data)
            for j in range(SPAN):
                for lane in range(0, cells, 128):
                    hj = h[j * c1 : (j + 1) * c1, lane : lane + 128]
                    scale = lax.rsqrt(jnp.sum(hj * hj, axis=0, keepdims=True) * (1.0 / c1) + 1e-6)
                    for q in range(c1 // 16):
                        x = hj[q * 16 : (q + 1) * 16] * scale * wide_gain[q * 16 : (q + 1) * 16, :]
                        u = x + x * jnp.tanh(x)
                        s_ref[first + j, q, ab, :, lane : lane + 128] = u.astype(BF16)

    def frame_of(unit):
        return (SPAN + unit) & (nframes - 1)

    def gather_latent(unit, acc):
        at = frame_of(unit) * c2
        return acc + dot(lat_rep[:, pl.ds(pl.multiple_of(at, c2), c2)], m_ref[unit & 1])

    def deep(unit, acc):
        g = dot(mid_perm[...], s_ref[frame_of(unit)].reshape(c1 * blocks, cells))
        for q in range(0, c2, 32):
            part = g[q : q + 32]
            m_ref[unit & 1, q : q + 32, :] = (part + part * jnp.tanh(part)).astype(BF16)
        return acc

    def deeps(t, acc):
        for i in range(units):
            unit = t * units + i
            acc = gather_latent(jnp.maximum(unit - 1, 0), acc)
            acc = deep(unit, acc)
        return acc

    chunk = swap.shape[0]
    per_chunk = (c1 // 16) // steps

    def opening(t, _):
        conv(0, t)
        for i in range(per_chunk):
            at = pl.ds(pl.multiple_of((t * per_chunk + i) * chunk, chunk), chunk)
            mid_perm[:, at] = dot(mid[:, at], swap[...]).astype(BF16)
        return 0

    loads[4].wait()
    loads[5].wait()
    lax.fori_loop(0, steps, opening, 0)

    loads[6].wait()
    repeat = (iota((features, latc), 0) >> shift_of(quads) == iota((features, latc), 1)).astype(BF16)
    lat_rep[...] = dot(repeat, lat[...]).astype(BF16)
    loads[7].wait()

    step_bits = shift_of(steps)

    def both(t, acc):
        conv(1 + (t >> step_bits), t & (steps - 1))
        return deeps(t, acc)

    middle = (groups - 2) * steps
    acc = lax.fori_loop(0, middle, both, jnp.zeros((features, cells), F32))

    def with_carry(t, acc):
        @pl.when(me > 0)
        def _():
            for p in range(pieces // steps):
                carry(t * (pieces // steps) + p).wait_recv()

        conv(groups - 1, t)
        return deeps(middle + t, acc)

    acc = lax.fori_loop(0, steps, with_carry, acc)

    acc = deeps(jnp.int32(middle + steps), acc)
    for extra in range(1, steps):
        acc = deeps(jnp.int32(middle + steps + extra), acc)
    latent = gather_latent(jnp.int32(nframes - 1), acc).astype(BF16)

    quad = iota((features, rows), 0) & (quads - 1)
    picked = jnp.zeros((features, rows), F32)
    for q in range(quads):
        picked = jnp.where(quad == q, dot(latent, pick[q]), picked)
    tag = jnp.where(iota((width - features, rows), 0) == 0, (place + 1).astype(F32), 0.0)
    rows_t = jnp.concatenate([picked, tag], axis=0).astype(BF16)
    payload = dot(select[...], rows_t, ((1,), (1,)))
    outbuf[...] = payload.reshape(n, cap, width)

    def exchange(k):
        to = wrap(me + k, n)
        return pltpu.make_async_remote_copy(
            src_ref=outbuf.at[to],
            dst_ref=inbuf.at[me],
            send_sem=send_sem.at[k],
            recv_sem=recv_sem.at[k],
            device_id={"tok": to},
            device_id_type=pl.DeviceIdType.MESH,
        )

    def send(k, _):
        exchange(k).start()
        return 0

    def finish(k, _):
        exchange(k).wait()
        return 0

    lax.fori_loop(1, n, send, 0)
    inbuf[me] = outbuf[me]
    lax.fori_loop(1, n, finish, 0)

    arrived = inbuf[...].reshape(slots, width)
    arrange = (arrived[:, features : features + 1] == (iota((slots, rows), 1) + 1).astype(F32)).astype(BF16)
    placed = dot(arrange, arrived.astype(BF16), ((0,), (0,)))
    out_ref[...] = placed[:, 0:features].astype(BF16)

    @pl.when(me < n - 1)
    def _():
        for p in range(pieces):
            carry(p).wait_send()


def per_device(n, frames, clip_lengths, slot_map, stem, time, gain, mid, lat, pe):
    nframes, cin, pos = frames.shape
    c1, c2, latc = stem.shape[0], mid.shape[0], lat.shape[0]
    blocks = mid.shape[1] // c1
    cells = pos // blocks
    side = int(round(cells**0.5))
    rows = slot_map.shape[0]
    features = pe.shape[0]
    width = 2 * features
    pieces = 4
    cap = -(-max(2, 2 * rows // n) // 8) * 8
    vmem = pltpu.VMEM
    anywhere = pl.BlockSpec(memory_space=pl.ANY)
    kspan = (SPAN + 2) * cin
    placed = pl.pallas_call(
        functools.partial(kernel, n, side),
        out_shape=jax.ShapeDtypeStruct((rows, features), BF16),
        in_specs=[pl.BlockSpec(memory_space=pltpu.SMEM)] + [anywhere] * 7,
        out_specs=pl.BlockSpec(memory_space=vmem),
        scratch_shapes=[
            vmem((1, rows), I32),
            vmem((1, c1), F32),
            vmem((nframes + 2, cin, pos), BF16),
            vmem((cin, c1), BF16),
            vmem(time.shape, BF16),
            vmem(mid.shape, BF16),
            vmem(lat.shape, BF16),
            vmem((SPAN * c1, kspan), F32),
            vmem((nframes // SPAN, SPAN * c1, kspan), BF16),
            vmem((c1, 128), F32),
            vmem((16 * blocks, 16 * blocks), BF16),
            vmem(mid.shape, BF16),
            vmem((features, lat.shape[1]), BF16),
            vmem((4, cells, rows), BF16),
            vmem((n * cap, rows), BF16),
            vmem((nframes, c1 // 16, blocks, 16, cells), BF16),
            vmem((2, c2, cells), BF16),
            vmem((n, cap, width), F32),
            vmem((n, cap, width), F32),
            pltpu.SemaphoreType.DMA((8,)),
            pltpu.SemaphoreType.DMA((pieces,)),
            pltpu.SemaphoreType.DMA((pieces,)),
            pltpu.SemaphoreType.DMA((n,)),
            pltpu.SemaphoreType.DMA((n,)),
        ],
        compiler_params=pltpu.CompilerParams(
            collective_id=0, has_side_effects=True, vmem_limit_bytes=56 * 2**20
        ),
        cost_estimate=pl.CostEstimate(
            flops=2 * nframes * (pos * c1 * 3 * cin + cells * c2 * c1 * blocks),
            bytes_accessed=2 * (nframes * cin * pos + mid.size + rows * features),
            transcendentals=nframes * pos * c1,
        ),
    )(clip_lengths, slot_map.reshape(1, rows), gain.reshape(1, c1), frames, stem.T, time, mid, lat)
    return jnp.dot(placed, pe, preferred_element_type=F32).astype(BF16)


def solution(mesh):
    sharded = P(("grp", "tok"), None, None)
    return jax.shard_map(
        functools.partial(per_device, mesh.shape["tok"]),
        mesh=mesh,
        in_specs=(sharded, P("grp"), P(("grp", "tok")), P(), P(), P(), P(), P(), P()),
        out_specs=P(("grp", "tok"), None),
        check_vma=False,
    )
```

```python
import functools

import jax
import jax.numpy as jnp
from jax import lax
from jax.experimental import pallas as pl
from jax.experimental.pallas import tpu as pltpu
from jax.sharding import PartitionSpec as P

F32 = jnp.float32
BF16 = jnp.bfloat16
I32 = jnp.int32
SPAN = 2


def iota(shape, dim):
    return lax.broadcasted_iota(I32, shape, dim)


def dot(a, b, contract=((1,), (0,))):
    return lax.dot_general(a, b, (contract, ((), ())), preferred_element_type=F32)


def wrap(index, size):
    return jnp.where(index >= size, index - size, index)


def shift_of(size):
    assert size & (size - 1) == 0
    return size.bit_length() - 1


def kernel(
    n, side, clip_ref, slot_hbm, gain_hbm, frames_hbm, stem_hbm, time_hbm, mid_hbm, lat_hbm,
    out_ref,
    slot, gain, frames, stem, time, mid, lat,
    toeplitz, masked, wide_gain, swap, mid_perm, lat_rep, pick, select, s_ref, m_ref, outbuf, inbuf,
    load_sem, carry_send, carry_recv, send_sem, recv_sem,
):
    me, grp = lax.axis_index("tok"), lax.axis_index("grp")
    nframes, cin, pos = frames_hbm.shape
    c1 = stem_hbm.shape[1]
    cells = side * side
    blocks = pos // cells
    c2 = mid_hbm.shape[0]
    latc = lat_hbm.shape[0]
    rows = slot_hbm.shape[1]
    cap = outbuf.shape[1]
    width = outbuf.shape[2]
    slots = n * cap
    quads = 4
    features = quads * latc
    pieces = carry_send.shape[0]
    steps = 2
    per_step = blocks // steps
    groups = nframes // SPAN

    loads = [
        pltpu.make_async_copy(stem_hbm, stem, load_sem.at[0]),
        pltpu.make_async_copy(time_hbm, time, load_sem.at[1]),
        pltpu.make_async_copy(gain_hbm, gain, load_sem.at[2]),
        pltpu.make_async_copy(slot_hbm, slot, load_sem.at[3]),
        pltpu.make_async_copy(frames_hbm.at[0:4], frames.at[2:6], load_sem.at[4]),
        pltpu.make_async_copy(mid_hbm, mid, load_sem.at[5]),
        pltpu.make_async_copy(lat_hbm, lat, load_sem.at[6]),
        pltpu.make_async_copy(frames_hbm.at[4:nframes], frames.at[6 : nframes + 2], load_sem.at[7]),
    ]
    barrier = pltpu.get_barrier_semaphore()

    def greet(k, _):
        pl.semaphore_signal(
            barrier, inc=1, device_id=(grp, wrap(me + k, n)), device_id_type=pl.DeviceIdType.MESH
        )
        return 0

    lax.fori_loop(1, n, greet, 0)

    for load in loads:
        load.start()

    @pl.when(me == 0)
    def _():
        frames[0:2] = jnp.zeros_like(frames[0:2])

    bits = shift_of(blocks)
    k_in, k_out = iota(swap.shape, 0), iota(swap.shape, 1)
    moved = ((k_in >> bits) == (k_out & 15)) & ((k_in & (blocks - 1)) == (k_out >> 4))
    swap[...] = jnp.where(moved, jnp.float32(0.5), jnp.float32(0.0)).astype(BF16)
    half = side // 2
    half_bits = shift_of(half)
    cell, row_id = iota((cells, rows), 0), iota((cells, rows), 1)
    for q in range(quads):
        a, b = q // 2, q % 2
        pick[q] = (cell == (2 * (row_id >> half_bits) + a) * side + 2 * (row_id & (half - 1)) + b).astype(BF16)

    pl.semaphore_wait(barrier, n - 1)

    wide_piece = pos // pieces

    def carry(p):
        at = pl.ds(pl.multiple_of(p * wide_piece, wide_piece), wide_piece)
        return pltpu.make_async_remote_copy(
            src_ref=frames_hbm.at[nframes - 2 : nframes, :, at],
            dst_ref=frames.at[0:2, :, at],
            send_sem=carry_send.at[p],
            recv_sem=carry_recv.at[p],
            device_id=(grp, wrap(me + 1, n)),
            device_id_type=pl.DeviceIdType.MESH,
        )

    @pl.when(me < n - 1)
    def _():
        for p in range(pieces):
            carry(p).start()

    start = jnp.int32(0)
    end = jnp.int32(0)
    live = jnp.int32(0)
    keep = jnp.float32(1.0)
    for c in range(clip_ref.shape[0]):
        length = clip_ref[c]
        start = end
        end = end + ((length + (nframes - 1)) >> shift_of(nframes))
        inside = jnp.logical_and(start <= me, me < end)
        live = jnp.where(inside, jnp.clip(length - nframes * (me - start), 0, nframes), live)
        keep = jnp.where(jnp.logical_and(inside, start == me), jnp.float32(0.0), keep)

    kspan = (SPAN + 2) * cin
    loads[0].wait()
    loads[1].wait()
    placed_stem = [
        dot(stem[...], (iota((cin, kspan), 1) == iota((cin, kspan), 0) + b * cin).astype(BF16), ((0,), (0,))).astype(BF16)
        for b in range(SPAN + 2)
    ]
    for j in range(SPAN):
        row = dot(time[2], placed_stem[j]) + dot(time[1], placed_stem[j + 1]) + dot(time[0], placed_stem[j + 2])
        toeplitz[j * c1 : (j + 1) * c1, :] = row
    column_id = iota((1, kspan), 1)
    for g in range(groups):
        first = (SPAN * (g + 1)) % nframes
        on = jnp.where(column_id < cin * (live - first + 2), jnp.float32(1.0), jnp.float32(0.0))
        on = jnp.where(column_id < cin * (2 - first), keep, on)
        masked[g] = (toeplitz[...] * on).astype(BF16)

    loads[2].wait()
    diagonal = iota((c1, c1), 0) == iota((c1, c1), 1)
    column = jnp.sum(jnp.where(diagonal, jnp.broadcast_to(gain[...], (c1, c1)), 0.0), axis=1, keepdims=True)
    wide_gain[...] = jnp.broadcast_to(0.5 * column, wide_gain.shape)

    loads[3].wait()
    row_bits = shift_of(rows)
    where_to = slot[...]
    target = where_to >> row_bits
    place = where_to & (rows - 1)
    onehot = iota((n, rows), 0) == target
    before = (iota((rows, rows), 0) < iota((rows, rows), 1)).astype(BF16)
    earlier = dot(onehot.astype(BF16), before)
    rank = jnp.sum(jnp.where(onehot, earlier, 0.0), axis=0, keepdims=True).astype(I32)
    select[...] = (iota((slots, rows), 0) == target * cap + rank).astype(BF16)

    m_ref[...] = jnp.zeros_like(m_ref)

    def conv(g, t):
        first = (SPAN * (g + 1)) & (nframes - 1)
        weight = masked[g]
        for i in range(per_step):
            ab = t * per_step + i
            at = pl.ds(pl.multiple_of(ab * cells, cells), cells)
            data = frames[pl.ds(first, SPAN + 2), :, at].reshape(kspan, cells)
            h = dot(weight, data)
            for j in range(SPAN):
                for lane in range(0, cells, 128):
                    hj = h[j * c1 : (j + 1) * c1, lane : lane + 128]
                    scale = lax.rsqrt(jnp.sum(hj * hj, axis=0, keepdims=True) * (1.0 / c1) + 1e-6)
                    for q in range(c1 // 16):
                        x = hj[q * 16 : (q + 1) * 16] * scale * wide_gain[q * 16 : (q + 1) * 16, :]
                        x = x.astype(BF16)
                        s_ref[first + j, q, ab, :, lane : lane + 128] = x + x * jnp.tanh(x)

    def frame_of(unit):
        return (SPAN + unit) & (nframes - 1)

    def gather_latent(unit, acc):
        at = frame_of(unit) * c2
        return acc + dot(lat_rep[:, pl.ds(pl.multiple_of(at, c2), c2)], m_ref[unit & 1])

    def deep(unit, acc):
        g = dot(mid_perm[...], s_ref[frame_of(unit)].reshape(c1 * blocks, cells))
        for q in range(0, c2, 32):
            part = g[q : q + 32].astype(BF16)
            m_ref[unit & 1, q : q + 32, :] = part + part * jnp.tanh(part)
        return acc

    chunk = swap.shape[0]
    per_chunk = (c1 // 16) // steps

    def opening(t, _):
        conv(0, t)
        for i in range(per_chunk):
            at = pl.ds(pl.multiple_of((t * per_chunk + i) * chunk, chunk), chunk)
            mid_perm[:, at] = dot(mid[:, at], swap[...]).astype(BF16)
        return 0

    loads[4].wait()
    loads[5].wait()
    lax.fori_loop(0, steps, opening, 0)

    loads[6].wait()
    repeat = (iota((features, latc), 0) >> shift_of(quads) == iota((features, latc), 1)).astype(BF16)
    lat_rep[...] = dot(repeat, lat[...]).astype(BF16)
    loads[7].wait()

    step_bits = shift_of(steps)

    def both(t, acc):
        acc = gather_latent(jnp.maximum(t - 1, 0), acc)
        conv(1 + (t >> step_bits), t & (steps - 1))
        return deep(t, acc)

    middle = (groups - 2) * steps
    acc = lax.fori_loop(0, middle, both, jnp.zeros((features, cells), F32))

    def with_carry(t, acc):
        @pl.when(me > 0)
        def _():
            for p in range(pieces // steps):
                carry(t * (pieces // steps) + p).wait_recv()

        acc = gather_latent(middle + t - 1, acc)
        conv(groups - 1, t)
        return deep(middle + t, acc)

    acc = lax.fori_loop(0, steps, with_carry, acc)

    def closing(t, acc):
        acc = gather_latent(middle + steps + t - 1, acc)
        return deep(middle + steps + t, acc)

    acc = lax.fori_loop(0, SPAN, closing, acc)
    latent = gather_latent(jnp.int32(nframes - 1), acc).astype(BF16)

    quad = iota((features, rows), 0) & (quads - 1)
    picked = jnp.zeros((features, rows), F32)
    for q in range(quads):
        picked = jnp.where(quad == q, dot(latent, pick[q]), picked)
    tag = jnp.where(iota((width - features, rows), 0) == 0, (place + 1).astype(F32), 0.0)
    rows_t = jnp.concatenate([picked, tag], axis=0).astype(BF16)
    payload = dot(select[...], rows_t, ((1,), (1,)))
    outbuf[...] = payload.reshape(n, cap, width)

    def exchange(k):
        to = wrap(me + k, n)
        return pltpu.make_async_remote_copy(
            src_ref=outbuf.at[to],
            dst_ref=inbuf.at[me],
            send_sem=send_sem.at[k],
            recv_sem=recv_sem.at[k],
            device_id=(grp, to),
            device_id_type=pl.DeviceIdType.MESH,
        )

    def send(k, _):
        exchange(k).start()
        return 0

    def finish(k, _):
        exchange(k).wait()
        return 0

    lax.fori_loop(1, n, send, 0)
    inbuf[me] = outbuf[me]
    lax.fori_loop(1, n, finish, 0)

    arrived = inbuf[...].reshape(slots, width)
    arrange = (arrived[:, features : features + 1] == (iota((slots, rows), 1) + 1).astype(F32)).astype(BF16)
    placed = dot(arrange, arrived.astype(BF16), ((0,), (0,)))
    out_ref[...] = placed[:, 0:features].astype(BF16)

    @pl.when(me < n - 1)
    def _():
        for p in range(pieces):
            carry(p).wait_send()


def per_device(n, frames, clip_lengths, slot_map, stem, time, gain, mid, lat, pe):
    nframes, cin, pos = frames.shape
    c1, c2, latc = stem.shape[0], mid.shape[0], lat.shape[0]
    blocks = mid.shape[1] // c1
    cells = pos // blocks
    side = int(round(cells**0.5))
    rows = slot_map.shape[0]
    features = pe.shape[0]
    width = 2 * features
    pieces = 4
    cap = -(-max(2, 2 * rows // n) // 8) * 8
    vmem = pltpu.VMEM
    anywhere = pl.BlockSpec(memory_space=pl.ANY)
    kspan = (SPAN + 2) * cin
    placed = pl.pallas_call(
        functools.partial(kernel, n, side),
        out_shape=jax.ShapeDtypeStruct((rows, features), BF16),
        in_specs=[pl.BlockSpec(memory_space=pltpu.SMEM)] + [anywhere] * 7,
        out_specs=pl.BlockSpec(memory_space=vmem),
        scratch_shapes=[
            vmem((1, rows), I32),
            vmem((1, c1), F32),
            vmem((nframes + 2, cin, pos), BF16),
            vmem((cin, c1), BF16),
            vmem(time.shape, BF16),
            vmem(mid.shape, BF16),
            vmem(lat.shape, BF16),
            vmem((SPAN * c1, kspan), F32),
            vmem((nframes // SPAN, SPAN * c1, kspan), BF16),
            vmem((c1, 128), F32),
            vmem((16 * blocks, 16 * blocks), BF16),
            vmem(mid.shape, BF16),
            vmem((features, lat.shape[1]), BF16),
            vmem((4, cells, rows), BF16),
            vmem((n * cap, rows), BF16),
            vmem((nframes, c1 // 16, blocks, 16, cells), BF16),
            vmem((2, c2, cells), BF16),
            vmem((n, cap, width), F32),
            vmem((n, cap, width), F32),
            pltpu.SemaphoreType.DMA((8,)),
            pltpu.SemaphoreType.DMA((pieces,)),
            pltpu.SemaphoreType.DMA((pieces,)),
            pltpu.SemaphoreType.DMA((n,)),
            pltpu.SemaphoreType.DMA((n,)),
        ],
        compiler_params=pltpu.CompilerParams(
            collective_id=0, has_side_effects=True, vmem_limit_bytes=56 * 2**20
        ),
        cost_estimate=pl.CostEstimate(
            flops=2 * nframes * (pos * c1 * 3 * cin + cells * c2 * c1 * blocks),
            bytes_accessed=2 * (nframes * cin * pos + mid.size + rows * features),
            transcendentals=nframes * pos * c1,
        ),
    )(clip_lengths, slot_map.reshape(1, rows), gain.reshape(1, c1), frames, stem.T, time, mid, lat)
    return jnp.dot(placed, pe, preferred_element_type=F32).astype(BF16)


def solution(mesh):
    sharded = P(("grp", "tok"), None, None)
    return jax.shard_map(
        functools.partial(per_device, mesh.shape["tok"]),
        mesh=mesh,
        in_specs=(sharded, P("grp"), P(("grp", "tok")), P(), P(), P(), P(), P(), P()),
        out_specs=P(("grp", "tok"), None),
        check_vma=False,
    )
```

```python
import functools

import jax
import jax.numpy as jnp
from jax import lax
from jax.experimental import pallas as pl
from jax.experimental.pallas import tpu as pltpu
from jax.sharding import PartitionSpec as P

F32 = jnp.float32
BF16 = jnp.bfloat16
I32 = jnp.int32
SPAN = 2


def iota(shape, dim):
    return lax.broadcasted_iota(I32, shape, dim)


def dot(a, b, contract=((1,), (0,))):
    return lax.dot_general(a, b, (contract, ((), ())), preferred_element_type=F32)


def wrap(index, size):
    return jnp.where(index >= size, index - size, index)


def shift_of(size):
    assert size & (size - 1) == 0
    return size.bit_length() - 1


def kernel(
    n, side, clip_ref, slot_hbm, gain_hbm, frames_hbm, stem_hbm, time_hbm, mid_hbm, lat_hbm,
    out_ref,
    slot, gain, frames, stem, time, mid, lat,
    toeplitz, masked, wide_gain, swap, mid_perm, lat_rep, pick, select, s_ref, m_ref, partial, outbuf, inbuf,
    load_sem, carry_send, carry_recv, send_sem, recv_sem,
):
    me, grp = lax.axis_index("tok"), lax.axis_index("grp")
    nframes, cin, pos = frames_hbm.shape
    c1 = stem_hbm.shape[1]
    cells = side * side
    blocks = pos // cells
    c2 = mid_hbm.shape[0]
    latc = lat_hbm.shape[0]
    rows = slot_hbm.shape[1]
    cap = outbuf.shape[1]
    width = outbuf.shape[2]
    slots = n * cap
    quads = 4
    features = quads * latc
    pieces = carry_send.shape[0]
    steps = 2
    per_step = blocks // steps
    groups = nframes // SPAN

    loads = [
        pltpu.make_async_copy(stem_hbm, stem, load_sem.at[0]),
        pltpu.make_async_copy(time_hbm, time, load_sem.at[1]),
        pltpu.make_async_copy(gain_hbm, gain, load_sem.at[2]),
        pltpu.make_async_copy(slot_hbm, slot, load_sem.at[3]),
        pltpu.make_async_copy(frames_hbm.at[0:4], frames.at[2:6], load_sem.at[4]),
        pltpu.make_async_copy(mid_hbm, mid, load_sem.at[5]),
        pltpu.make_async_copy(lat_hbm, lat, load_sem.at[6]),
        pltpu.make_async_copy(frames_hbm.at[4:nframes], frames.at[6 : nframes + 2], load_sem.at[7]),
    ]
    barrier = pltpu.get_barrier_semaphore()

    def greet(k, _):
        pl.semaphore_signal(
            barrier, inc=1, device_id=(grp, wrap(me + k, n)), device_id_type=pl.DeviceIdType.MESH
        )
        return 0

    lax.fori_loop(1, n, greet, 0)

    for load in loads:
        load.start()

    @pl.when(me == 0)
    def _():
        frames[0:2] = jnp.zeros_like(frames[0:2])

    bits = shift_of(blocks)
    k_in, k_out = iota(swap.shape, 0), iota(swap.shape, 1)
    moved = ((k_in >> bits) == (k_out & 15)) & ((k_in & (blocks - 1)) == (k_out >> 4))
    swap[...] = jnp.where(moved, jnp.float32(0.5), jnp.float32(0.0)).astype(BF16)
    half = side // 2
    half_bits = shift_of(half)
    cell, row_id = iota((cells, rows), 0), iota((cells, rows), 1)
    for q in range(quads):
        a, b = q // 2, q % 2
        pick[q] = (cell == (2 * (row_id >> half_bits) + a) * side + 2 * (row_id & (half - 1)) + b).astype(BF16)

    pl.semaphore_wait(barrier, n - 1)

    wide_piece = pos // pieces

    def carry(p):
        at = pl.ds(pl.multiple_of(p * wide_piece, wide_piece), wide_piece)
        return pltpu.make_async_remote_copy(
            src_ref=frames_hbm.at[nframes - 2 : nframes, :, at],
            dst_ref=frames.at[0:2, :, at],
            send_sem=carry_send.at[p],
            recv_sem=carry_recv.at[p],
            device_id=(grp, wrap(me + 1, n)),
            device_id_type=pl.DeviceIdType.MESH,
        )

    @pl.when(me < n - 1)
    def _():
        for p in range(pieces):
            carry(p).start()

    start = jnp.int32(0)
    end = jnp.int32(0)
    live = jnp.int32(0)
    keep = jnp.float32(1.0)
    for c in range(clip_ref.shape[0]):
        length = clip_ref[c]
        start = end
        end = end + ((length + (nframes - 1)) >> shift_of(nframes))
        inside = jnp.logical_and(start <= me, me < end)
        live = jnp.where(inside, jnp.clip(length - nframes * (me - start), 0, nframes), live)
        keep = jnp.where(jnp.logical_and(inside, start == me), jnp.float32(0.0), keep)

    kspan = (SPAN + 2) * cin
    loads[0].wait()
    loads[1].wait()
    placed_stem = [
        dot(stem[...], (iota((cin, kspan), 1) == iota((cin, kspan), 0) + b * cin).astype(BF16), ((0,), (0,))).astype(BF16)
        for b in range(SPAN + 2)
    ]
    for j in range(SPAN):
        row = dot(time[2], placed_stem[j]) + dot(time[1], placed_stem[j + 1]) + dot(time[0], placed_stem[j + 2])
        toeplitz[j * c1 : (j + 1) * c1, :] = row
    column_id = iota((1, kspan), 1)
    for g in range(groups):
        first = (SPAN * (g + 1)) % nframes
        on = jnp.where(column_id < cin * (live - first + 2), jnp.float32(1.0), jnp.float32(0.0))
        on = jnp.where(column_id < cin * (2 - first), keep, on)
        masked[g] = (toeplitz[...] * on).astype(BF16)

    loads[2].wait()
    diagonal = iota((c1, c1), 0) == iota((c1, c1), 1)
    column = jnp.sum(jnp.where(diagonal, jnp.broadcast_to(gain[...], (c1, c1)), 0.0), axis=1, keepdims=True)
    wide_gain[...] = jnp.broadcast_to(0.5 * column, wide_gain.shape)

    loads[3].wait()
    row_bits = shift_of(rows)
    where_to = slot[...]
    target = where_to >> row_bits
    place = where_to & (rows - 1)
    onehot = iota((n, rows), 0) == target
    before = (iota((rows, rows), 0) < iota((rows, rows), 1)).astype(BF16)
    earlier = dot(onehot.astype(BF16), before)
    rank = jnp.sum(jnp.where(onehot, earlier, 0.0), axis=0, keepdims=True).astype(I32)
    select[...] = (iota((slots, rows), 0) == target * cap + rank).astype(BF16)

    m_ref[...] = jnp.zeros_like(m_ref)

    def conv(g, t):
        first = (SPAN * (g + 1)) & (nframes - 1)
        weight = masked[g]
        for i in range(per_step):
            ab = t * per_step + i
            at = pl.ds(pl.multiple_of(ab * cells, cells), cells)
            data = frames[pl.ds(first, SPAN + 2), :, at].reshape(kspan, cells)
            h = dot(weight, data)
            for j in range(SPAN):
                for lane in range(0, cells, 128):
                    hj = h[j * c1 : (j + 1) * c1, lane : lane + 128]
                    scale = lax.rsqrt(jnp.sum(hj * hj, axis=0, keepdims=True) * (1.0 / c1) + 1e-6)
                    for q in range(c1 // 16):
                        x = hj[q * 16 : (q + 1) * 16] * scale * wide_gain[q * 16 : (q + 1) * 16, :]
                        s_ref[first + j, t, q, i, :, lane : lane + 128] = (x + x * jnp.tanh(x)).astype(BF16)

    def frame_of(unit):
        return (SPAN + unit) & (nframes - 1)

    def gather_latent(unit, acc):
        at = frame_of(unit) * c2
        return acc + dot(lat_rep[:, pl.ds(pl.multiple_of(at, c2), c2)], m_ref[unit & 1])

    def silu_to_m(unit, g):
        for q in range(0, c2, 32):
            part = g[q : q + 32]
            m_ref[unit & 1, q : q + 32, :] = (part + part * jnp.tanh(part)).astype(BF16)

    def deep(unit, acc):
        acc = gather_latent(jnp.maximum(unit - 1, 0), acc)
        silu_to_m(unit, dot(mid_perm[...], s_ref[frame_of(unit)].reshape(c1 * blocks, cells)))
        return acc

    depth = c1 * per_step

    def deep_part(frame, t):
        return dot(mid_perm[:, t * depth : (t + 1) * depth], s_ref[frame, t].reshape(depth, cells))

    chunk = swap.shape[0]
    per_chunk = (c1 // 16) // steps

    def opening(t, _):
        conv(0, t)
        for i in range(per_chunk):
            q = t * per_chunk + i
            ordered = dot(mid[:, pl.ds(pl.multiple_of(q * chunk, chunk), chunk)], swap[...]).astype(BF16)
            part = chunk // steps
            for side_by in range(steps):
                at = pl.ds(pl.multiple_of(side_by * depth + q * part, part), part)
                mid_perm[:, at] = ordered[:, side_by * part : (side_by + 1) * part]
        return 0

    loads[4].wait()
    loads[5].wait()
    lax.fori_loop(0, steps, opening, 0)

    loads[6].wait()
    repeat = (iota((features, latc), 0) >> shift_of(quads) == iota((features, latc), 1)).astype(BF16)
    lat_rep[...] = dot(repeat, lat[...]).astype(BF16)
    loads[7].wait()

    step_bits = shift_of(steps)

    def both(t, acc):
        conv(1 + (t >> step_bits), t & (steps - 1))
        return deep(t, acc)

    middle = (groups - 2) * steps
    acc = lax.fori_loop(0, middle, both, jnp.zeros((features, cells), F32))

    acc = lax.fori_loop(middle, middle + SPAN, deep, acc)

    for t in range(steps):

        @pl.when(me > 0)
        def _(t=t):
            for p in range(pieces // steps):
                carry(t * (pieces // steps) + p).wait_recv()

        conv(groups - 1, t)
        if t < steps - 1:
            for j in range(SPAN):
                part = deep_part(j, t)
                partial[j] = part if t == 0 else partial[j] + part
    for j in range(SPAN):
        unit = nframes - SPAN + j
        acc = gather_latent(jnp.int32(unit - 1), acc)
        silu_to_m(unit, partial[j] + deep_part(j, steps - 1))
    latent = gather_latent(jnp.int32(nframes - 1), acc).astype(BF16)

    quad = iota((features, rows), 0) & (quads - 1)
    picked = jnp.zeros((features, rows), F32)
    for q in range(quads):
        picked = jnp.where(quad == q, dot(latent, pick[q]), picked)
    tag = jnp.where(iota((width - features, rows), 0) == 0, (place + 1).astype(F32), 0.0)
    rows_t = jnp.concatenate([picked, tag], axis=0).astype(BF16)
    payload = dot(select[...], rows_t, ((1,), (1,)))
    outbuf[...] = payload.reshape(n, cap, width)

    def exchange(k):
        to = wrap(me + k, n)
        return pltpu.make_async_remote_copy(
            src_ref=outbuf.at[to],
            dst_ref=inbuf.at[me],
            send_sem=send_sem.at[k],
            recv_sem=recv_sem.at[k],
            device_id=(grp, to),
            device_id_type=pl.DeviceIdType.MESH,
        )

    def send(k, _):
        exchange(k).start()
        return 0

    def finish(k, _):
        exchange(k).wait()
        return 0

    lax.fori_loop(1, n, send, 0)
    inbuf[me] = outbuf[me]
    lax.fori_loop(1, n, finish, 0)

    arrived = inbuf[...].reshape(slots, width)
    arrange = (arrived[:, features : features + 1] == (iota((slots, rows), 1) + 1).astype(F32)).astype(BF16)
    placed = dot(arrange, arrived.astype(BF16), ((0,), (0,)))
    out_ref[...] = placed[:, 0:features].astype(BF16)

    @pl.when(me < n - 1)
    def _():
        for p in range(pieces):
            carry(p).wait_send()


def per_device(n, frames, clip_lengths, slot_map, stem, time, gain, mid, lat, pe):
    nframes, cin, pos = frames.shape
    c1, c2, latc = stem.shape[0], mid.shape[0], lat.shape[0]
    blocks = mid.shape[1] // c1
    cells = pos // blocks
    side = int(round(cells**0.5))
    rows = slot_map.shape[0]
    features = pe.shape[0]
    width = 2 * features
    pieces = 4
    cap = -(-max(2, 2 * rows // n) // 8) * 8
    vmem = pltpu.VMEM
    anywhere = pl.BlockSpec(memory_space=pl.ANY)
    kspan = (SPAN + 2) * cin
    placed = pl.pallas_call(
        functools.partial(kernel, n, side),
        out_shape=jax.ShapeDtypeStruct((rows, features), BF16),
        in_specs=[pl.BlockSpec(memory_space=pltpu.SMEM)] + [anywhere] * 7,
        out_specs=pl.BlockSpec(memory_space=vmem),
        scratch_shapes=[
            vmem((1, rows), I32),
            vmem((1, c1), F32),
            vmem((nframes + 2, cin, pos), BF16),
            vmem((cin, c1), BF16),
            vmem(time.shape, BF16),
            vmem(mid.shape, BF16),
            vmem(lat.shape, BF16),
            vmem((SPAN * c1, kspan), F32),
            vmem((nframes // SPAN, SPAN * c1, kspan), BF16),
            vmem((c1, 128), F32),
            vmem((16 * blocks, 16 * blocks), BF16),
            vmem(mid.shape, BF16),
            vmem((features, lat.shape[1]), BF16),
            vmem((4, cells, rows), BF16),
            vmem((n * cap, rows), BF16),
            vmem((nframes, 2, c1 // 16, blocks // 2, 16, cells), BF16),
            vmem((2, c2, cells), BF16),
            vmem((SPAN, c2, cells), F32),
            vmem((n, cap, width), F32),
            vmem((n, cap, width), F32),
            pltpu.SemaphoreType.DMA((8,)),
            pltpu.SemaphoreType.DMA((pieces,)),
            pltpu.SemaphoreType.DMA((pieces,)),
            pltpu.SemaphoreType.DMA((n,)),
            pltpu.SemaphoreType.DMA((n,)),
        ],
        compiler_params=pltpu.CompilerParams(
            collective_id=0, has_side_effects=True, vmem_limit_bytes=56 * 2**20
        ),
        cost_estimate=pl.CostEstimate(
            flops=2 * nframes * (pos * c1 * 3 * cin + cells * c2 * c1 * blocks),
            bytes_accessed=2 * (nframes * cin * pos + mid.size + rows * features),
            transcendentals=nframes * pos * c1,
        ),
    )(clip_lengths, slot_map.reshape(1, rows), gain.reshape(1, c1), frames, stem.T, time, mid, lat)
    return jnp.dot(placed, pe, preferred_element_type=F32).astype(BF16)


def solution(mesh):
    sharded = P(("grp", "tok"), None, None)
    return jax.shard_map(
        functools.partial(per_device, mesh.shape["tok"]),
        mesh=mesh,
        in_specs=(sharded, P("grp"), P(("grp", "tok")), P(), P(), P(), P(), P(), P()),
        out_specs=P(("grp", "tok"), None),
        check_vma=False,
    )
```
